512 devices in a mesh: loop: 64 (over x_hi, z, core), pool: 8 (over x_lo, y).
Axes of the slice: x: 4 (x_hi: 2, x_lo: 2; x = x_hi * 2 + x_lo), y: 4, z: 16, core: 2. Of those that a mesh axis runs over, the one named last changes fastest.
Arguments:
- picture_embedding_raw: bfloat16 [65536, 1152], P(('loop', 'pool')), may hold values from -0.1796875 to 0.1796875
- caption_embedding_raw: bfloat16 [65536, 1152], P(('loop', 'pool')), may hold values from -0.1796875 to 0.1796875
- score_sharpness: float32 [1], replicated, may hold values from 8 to 12
- score_shift_term: float32 [1], replicated, may hold values from -6 to -4
Outputs:
- image_grad: float32 [65536, 1152], P(('loop', 'pool'))
- text_grad: float32 [65536, 1152], P(('loop', 'pool'))
The draws below stay inside these ranges and needn't reach their ends.
All inputs are finite; a program needn't handle non-finite values.
Results may differ from the reference program's by a relative error of at most 0.0095.
Values may be sent and summed in bfloat16 or wider, within the bound.
A program may use at most 64 MiB of HBM per device.

```python
import jax
import jax.numpy as jnp
from jax import lax

D = 1152
ROWS = 128
STEPS = 4
TOKENS = 65536
N_LOOP = 64
N_POOL = 8


def level_of(stream_key, shape, cuts, least, largest):
    factor_of = 1.0
    for dim, parts in cuts:
        draws = jax.random.uniform(jax.random.fold_in(jax.random.fold_in(stream_key, 6), dim), (parts,), jnp.float32, least / len(cuts), largest / len(cuts))
        factor_of = factor_of * jnp.repeat(jnp.exp(draws), shape[dim] // parts).reshape((-1,) + (1,) * (len(shape) - 1 - dim))
    return factor_of


def centred(own_key, dims, deviation, most, split=(), kind=jnp.bfloat16):
    drawn = deviation * jax.random.normal(own_key, dims, jnp.float32)
    if split:
        drawn = drawn * level_of(own_key, dims, split, -0.22, 0.18)
    return jnp.clip(drawn, -most, most).astype(kind)


def setup_inputs(seed: int = 0) -> dict:
    keys = jax.random.split(jax.random.key(seed), 5)
    picture_embedding_raw = centred(keys[0], (TOKENS, D), 0.03, 0.1796875, ((0, 512),))
    caption_embedding_raw = centred(keys[1], (TOKENS, D), 0.03, 0.1796875, ((0, 512),))
    score_sharpness = jnp.clip(jax.random.uniform(keys[2], (1,), jnp.float32, 8.0, 12.0), 8.0, 12.0)
    score_shift_term = jnp.clip(jax.random.uniform(keys[3], (1,), jnp.float32, -6.0, -4.0), -6.0, -4.0)
    return {"picture_embedding_raw": picture_embedding_raw, "caption_embedding_raw": caption_embedding_raw, "score_sharpness": score_sharpness, "score_shift_term": score_shift_term}


epsilon_norm = 1e-06

def normalize(values):
    wide = values.astype(jnp.float32)
    inverse = lax.rsqrt(lax.optimization_barrier(jnp.sum(wide * wide, axis=-1, keepdims=True)) + epsilon_norm)
    return (wide * inverse, inverse)

def normalizer_reverse_pass(unit_rows, inverse, grad_hat):
    inner = lax.optimization_barrier(jnp.sum(unit_rows * grad_hat, axis=-1, keepdims=True))
    return inverse * (grad_hat - unit_rows * inner)

def reference(picture_embedding_raw, caption_embedding_raw, score_sharpness, score_shift_term):
    group_rows = N_POOL * ROWS
    image_unit, image_inverse = normalize(picture_embedding_raw)
    text_unit, text_inverse = normalize(caption_embedding_raw)
    image_groups = image_unit.astype(jnp.bfloat16).reshape(N_LOOP, group_rows, D)
    text_groups = text_unit.astype(jnp.bfloat16).reshape(N_LOOP, group_rows, D)
    smoothing_multiplier = score_sharpness[0]
    logit_offset_bias = score_shift_term[0]
    diagonal_mask = (jnp.arange(group_rows)[:, None] == jnp.arange(group_rows)[None, :]).astype(jnp.float32)

    def per_group(text_totals, group_index):
        image_tile_rows = image_groups[group_index]
        partial_value = jnp.zeros((N_POOL, group_rows, D), jnp.float32)
        for offset in range(1 - STEPS, STEPS):
            partner = ((group_index + offset) % N_LOOP).astype(jnp.int32)
            text_tile_rows = text_groups[partner]
            pair_logit_matrix = smoothing_multiplier * jnp.dot(image_tile_rows, text_tile_rows.T, preferred_element_type=jnp.float32) + logit_offset_bias
            label_sign = diagonal_mask if offset == 0 else 0.0
            weight_brain_float = ((jax.nn.sigmoid(pair_logit_matrix) - label_sign) * smoothing_multiplier).astype(jnp.bfloat16)
            partial_value = partial_value + jnp.einsum('iqr,qrd->qid', weight_brain_float.reshape(group_rows, N_POOL, ROWS).astype(jnp.float32), text_tile_rows.reshape(N_POOL, ROWS, D).astype(jnp.float32))
            text_part = jnp.dot(weight_brain_float.T, image_tile_rows, preferred_element_type=jnp.float32)
            text_totals = text_totals.at[partner].add(text_part)
        rounded = lax.optimization_barrier(partial_value.astype(jnp.bfloat16))
        return (text_totals, lax.optimization_barrier(jnp.sum(rounded.astype(jnp.float32), axis=0)))
    initial_sums = jnp.zeros((N_LOOP, group_rows, D), jnp.float32)
    text_totals, image_hat_grad = lax.scan(per_group, initial_sums, jnp.arange(N_LOOP, dtype=jnp.int32))
    image_grad = normalizer_reverse_pass(image_unit, image_inverse, image_hat_grad.reshape(-1, D))
    text_grad = normalizer_reverse_pass(text_unit, text_inverse, text_totals.reshape(-1, D))
    return (image_grad, text_grad)
```

```python
import jax
import jax.numpy as jnp
from jax import lax
from jax.experimental import pallas as pl
from jax.experimental.pallas import tpu as pltpu
from jax.sharding import PartitionSpec as P

MESH = pl.DeviceIdType.MESH
epsilon_norm = 1e-06

STEPS = 4
REACH = STEPS - 1
TEXTS = 2 * REACH + 1

COPIES = (
    "x", "own+", "own-", "part+", "part-", "fwd+", "fwd-", "pfwd+", "pfwd-",
    "tsib", "tz+", "tz-", "tfar", "tsib+", "tsib-",
    "half+", "half-", "phalf+", "phalf-", "pfull+", "pfull-", "full+", "full-", "xsum",
    "gsib", "gsib+", "gsib-", "gz+", "gz-", "gfar",
)
NUMBER = {name: i for i, name in enumerate(COPIES)}


def inverse_norm(wide):
    return lax.rsqrt(jnp.sum(wide * wide, axis=-1, keepdims=True) + epsilon_norm)


def kernel(
    sharp_ref, shift_ref, pic_ref, cap_ref, pic_out, cap_out,
    img, txt, weights, part, tgrad, isend, ihalf, ifull, tsend, trecv, send_sem, recv_sem,
):
    rows, width = pic_ref.shape
    half = rows // 2
    n_loop = lax.axis_size("loop")
    group, cls = lax.axis_index("loop"), lax.axis_index("pool")
    sign = 1 - 2 * lax.rem(group, 2)
    n_y = lax.axis_size("pool") // 2
    x, y = cls // n_y, lax.rem(cls, n_y)
    x_dev = (group, (1 - x) * n_y + y)
    up = (group, x * n_y + lax.rem(y + 1, n_y))
    down = (group, x * n_y + lax.rem(y + n_y - 1, n_y))
    ahead = (lax.rem(group + 2, n_loop), cls)
    behind = (lax.rem(group + n_loop - 2, n_loop), cls)
    sibling = (group + sign, cls)
    far = (lax.rem(group + n_loop - 3 * sign, n_loop), cls)
    peers = (x_dev, up, down, ahead, behind, sibling, far)

    barrier = pltpu.get_barrier_semaphore()
    for peer in peers:
        pl.semaphore_signal(barrier, inc=1, device_id=peer, device_id_type=MESH)

    def block(ref, slot, start=0, size=rows):
        first = slot * rows + start
        if not isinstance(first, int):
            first = pl.multiple_of(first, 16)
        return ref.at[pl.ds(first, size)]

    copies = {}

    def send(name, src, dst, device):
        n = NUMBER[name]
        copies[name] = pltpu.make_async_remote_copy(
            src_ref=src, dst_ref=dst, send_sem=send_sem.at[n], recv_sem=recv_sem.at[n],
            device_id=device, device_id_type=MESH,
        )
        copies[name].start()

    def arrived(*names):
        for name in names:
            copies[name].wait_recv()

    sharp, shift = sharp_ref[0], shift_ref[0]

    def unit_of(ref):
        wide = ref[...].astype(jnp.float32)
        inverse = inverse_norm(wide)
        return wide * inverse, inverse

    img[0:rows] = unit_of(pic_ref)[0].astype(jnp.bfloat16)
    own_text = REACH * rows
    txt[own_text : own_text + rows] = unit_of(cap_ref)[0].astype(jnp.bfloat16)

    pl.semaphore_wait(barrier, len(peers))

    send("x", block(img, 0), block(img, 1), x_dev)
    send("own+", block(img, 0), block(img, 3), up)
    send("own-", block(img, 0), block(img, 2), down)
    send("tsib", block(txt, REACH), block(txt, REACH - sign), sibling)
    send("tz+", block(txt, REACH), block(txt, REACH - 2), ahead)
    send("tz-", block(txt, REACH), block(txt, REACH + 2), behind)
    send("tfar", block(txt, REACH), block(txt, REACH + 3 * sign), far)

    arrived("x")
    send("part+", block(img, 1), block(img, 5), up)
    send("part-", block(img, 1), block(img, 4), down)
    arrived("own+", "own-")
    send("fwd+", block(img, 3, 0, half), block(img, 6, 0, half), up)
    send("fwd-", block(img, 2, half, half), block(img, 6, half, half), down)
    arrived("tz+", "tz-")
    send("tsib-", block(txt, REACH - 2), block(txt, REACH - 2 - sign), sibling)
    send("tsib+", block(txt, REACH + 2), block(txt, REACH + 2 - sign), sibling)
    arrived("tsib", "tsib-", "tsib+", "tfar")

    def score(pair):
        first = 2 * pair * rows
        here = pl.ds(first, 2 * rows)
        dots = lax.dot_general(
            img[here], txt[...], (((1,), (1,)), ((), ())), preferred_element_type=jnp.float32
        )
        chance = 1.0 / (1.0 + jnp.exp(-(sharp * dots + shift)))
        if pair == 0:
            i = lax.broadcasted_iota(jnp.int32, chance.shape, 0)
            j = lax.broadcasted_iota(jnp.int32, chance.shape, 1)
            chance = chance - ((i + own_text == j) & (i < rows)).astype(jnp.float32)
        weight = (sharp * chance).astype(jnp.bfloat16)
        weights[here] = weight
        part[here] = jnp.dot(weight, txt[...], preferred_element_type=jnp.float32)

    def text_grad(first, size):
        here = pl.ds(first * rows, size * rows)
        return lax.dot_general(
            weights[here], img[here], (((0,), (0,)), ((), ())), preferred_element_type=jnp.float32
        )

    score(0)
    score(1)
    arrived("part+", "part-")
    send("pfwd+", block(img, 5, 0, half), block(img, 7, 0, half), up)
    send("pfwd-", block(img, 4, half, half), block(img, 7, half, half), down)
    score(2)
    tgrad[...] = text_grad(0, 6)
    arrived("fwd+", "fwd-", "pfwd+", "pfwd-")
    score(3)

    def take(slot, start=0, size=rows):
        return part[slot * rows + start : slot * rows + start + size]

    def put(slot, value, start=0):
        first = slot * rows + start
        isend[first : first + value.shape[0]] = value.astype(jnp.bfloat16)

    put(6, take(6))
    put(7, take(7))
    send("phalf+", block(isend, 7, 0, half), block(ihalf, 0, 0, half), up)
    send("phalf-", block(isend, 7, half, half), block(ihalf, 0, half, half), down)
    send("half+", block(isend, 6, 0, half), block(ihalf, 1, 0, half), up)
    send("half-", block(isend, 6, half, half), block(ihalf, 1, half, half), down)

    tgrad[...] += text_grad(6, 2)

    def grad_rows(slot):
        return tgrad[pl.ds(pl.multiple_of(slot * rows, rows), rows)]

    def put_text(n, value):
        tsend[n * rows : (n + 1) * rows] = value.astype(jnp.bfloat16)

    def got_text(n):
        return trecv[n * rows : (n + 1) * rows].astype(jnp.float32)

    put_text(1, grad_rows(REACH + sign - 2))
    send("gsib-", block(tsend, 1), block(trecv, 1), sibling)
    put_text(2, grad_rows(REACH + sign + 2))
    send("gsib+", block(tsend, 2), block(trecv, 2), sibling)
    put_text(5, grad_rows(REACH - 3 * sign))
    send("gfar", block(tsend, 5), block(trecv, 5), far)
    put_text(0, grad_rows(REACH + sign))
    send("gsib", block(tsend, 0), block(trecv, 0), sibling)

    def got_half(n, start):
        first = n * rows + start
        return ihalf[first : first + half].astype(jnp.float32)

    arrived("phalf+", "phalf-")
    put(4, take(4, 0, half) + got_half(0, 0))
    put(4, take(4, half, half), half)
    send("pfull+", block(isend, 4), block(ifull, 0), up)
    put(5, take(5, 0, half))
    put(5, take(5, half, half) + got_half(0, half), half)
    send("pfull-", block(isend, 5), block(ifull, 1), down)

    arrived("gsib-")
    put_text(3, grad_rows(REACH - 2) + got_text(1))
    send("gz-", block(tsend, 3), block(trecv, 4), behind)
    arrived("gsib+")
    put_text(4, grad_rows(REACH + 2) + got_text(2))
    send("gz+", block(tsend, 4), block(trecv, 3), ahead)

    arrived("half+", "half-")
    put(2, take(2, 0, half) + got_half(1, 0))
    put(2, take(2, half, half), half)
    send("full+", block(isend, 2), block(ifull, 2), up)
    put(3, take(3, 0, half))
    put(3, take(3, half, half) + got_half(1, half), half)
    send("full-", block(isend, 3), block(ifull, 3), down)

    def got_full(n):
        return ifull[n * rows : (n + 1) * rows].astype(jnp.float32)

    def back(ref, grad_hat):
        unit, inverse = unit_of(ref)
        inner = jnp.sum(unit * grad_hat, axis=-1, keepdims=True)
        return inverse * (grad_hat - unit * inner)

    arrived("pfull+", "pfull-")
    put(1, take(1) + got_full(0) + got_full(1))
    send("xsum", block(isend, 1), block(ifull, 4), x_dev)

    arrived("gsib", "gz-", "gz+", "gfar")
    text_hat_grad = grad_rows(REACH) + got_text(0) + got_text(3) + got_text(4) + got_text(5)
    cap_out[...] = back(cap_ref, text_hat_grad)

    arrived("full+", "full-", "xsum")
    image_hat_grad = take(0) + got_full(2) + got_full(3) + got_full(4)
    pic_out[...] = back(pic_ref, image_hat_grad)

    for name in COPIES:
        copies[name].wait_send()


def shards(picture_embedding_raw, caption_embedding_raw, score_sharpness, score_shift_term):
    rows, width = picture_embedding_raw.shape
    n_pool = lax.axis_size("pool")
    result = jax.ShapeDtypeStruct((rows, width), jnp.float32)

    def blocks(count, dtype=jnp.bfloat16):
        return pltpu.VMEM((count * rows, width), dtype)

    vmem = pl.BlockSpec(memory_space=pltpu.VMEM)
    smem = pl.BlockSpec(memory_space=pltpu.SMEM)
    return pl.pallas_call(
        kernel,
        out_shape=(result, result),
        in_specs=[smem, smem, vmem, vmem],
        out_specs=(vmem, vmem),
        scratch_shapes=[
            blocks(n_pool),
            blocks(TEXTS),
            pltpu.VMEM((n_pool * rows, TEXTS * rows), jnp.bfloat16),
            blocks(n_pool, jnp.float32),
            blocks(TEXTS, jnp.float32),
            blocks(n_pool),
            blocks(2),
            blocks(5),
            blocks(6),
            blocks(6),
            pltpu.SemaphoreType.DMA((len(COPIES),)),
            pltpu.SemaphoreType.DMA((len(COPIES),)),
        ],
        compiler_params=pltpu.CompilerParams(
            collective_id=0, has_side_effects=True, vmem_limit_bytes=56 * 2**20
        ),
    )(score_sharpness, score_shift_term, picture_embedding_raw, caption_embedding_raw)


def solution(mesh):
    return jax.shard_map(
        shards,
        mesh=mesh,
        in_specs=(P(("loop", "pool"), None), P(("loop", "pool"), None), P(), P()),
        out_specs=(P(("loop", "pool"), None), P(("loop", "pool"), None)),
        check_vma=False,
    )
```

```python
import jax
import jax.numpy as jnp
from jax import lax
from jax.experimental import pallas as pl
from jax.experimental.pallas import tpu as pltpu
from jax.sharding import PartitionSpec as P

MESH = pl.DeviceIdType.MESH
epsilon_norm = 1e-06

TEXTS = 7
EARLY = 4

COPIES = (
    "x0", "x1", "own+0", "own+1", "own-0", "own-1", "part+0", "part+1", "part-0", "part-1",
    "fwd+", "fwd-", "pfwd+", "pfwd-",
    "tsib", "tfirst", "tsecond", "tfar", "tsib1", "tsib2",
    "half+", "half-", "phalf+", "phalf-", "pfull+0", "pfull+1", "pfull-0", "pfull-1",
    "full+0", "full+1", "full-0", "full-1", "xsum",
    "gsib", "gsib1", "gsib2", "gfirst", "gsecond", "gfar",
)
NUMBER = {name: i for i, name in enumerate(COPIES)}


def inverse_norm(wide):
    return lax.rsqrt(jnp.sum(wide * wide, axis=-1, keepdims=True) + epsilon_norm)


def unit_of(ref):
    wide = ref[...].astype(jnp.float32)
    inverse = inverse_norm(wide)
    return wide * inverse, inverse


def kernel(
    sharp_ref, shift_ref, pic_ref, cap_ref, pic_out, cap_out,
    pic, cap, img, txt, weights, part, tgrad, isend, ihalf, ifull, tsend, trecv,
    send_sem, recv_sem, load_sem,
):
    rows, width = pic_ref.shape
    loads = [
        pltpu.make_async_copy(ref, dst, load_sem.at[n])
        for n, (ref, dst) in enumerate(((pic_ref, pic), (cap_ref, cap)))
    ]
    for load in loads:
        load.start()
    half = rows // 2
    n_loop = lax.axis_size("loop")
    n_z = n_loop // 4
    group, cls = lax.axis_index("loop"), lax.axis_index("pool")
    sign = 1 - 2 * lax.rem(group, 2)
    z = lax.rem(group // 2, n_z)
    n_y = lax.axis_size("pool") // 2
    x, y = cls // n_y, lax.rem(cls, n_y)
    x_dev = (group, (1 - x) * n_y + y)
    up = (group, x * n_y + lax.rem(y + 1, n_y))
    down = (group, x * n_y + lax.rem(y + n_y - 1, n_y))
    toward = jnp.where(z == n_z - 1, -2, 2)
    first = (lax.rem(group + n_loop + toward, n_loop), cls)
    at_first = jnp.where(z >= n_z - 2, 0, 1)
    across = (z == 0) | (z == n_z - 1)
    at_second = jnp.where(across, 1, 0)
    sibling = (group + sign, cls)
    far_across = jnp.where(sign > 0, z == 0, z == n_z - 1)
    by_first = sign * 2 == toward
    mirror = (1 - x) * n_y + y
    second = (lax.rem(group + n_loop - toward, n_loop), jnp.where(across, mirror, cls))
    far = (lax.rem(group + n_loop - sign, n_loop), jnp.where(far_across, mirror, cls))
    low = z == 0
    beyond = across.astype(jnp.int32) + far_across.astype(jnp.int32)

    barrier = pltpu.get_barrier_semaphore()

    def greet(peer):
        pl.semaphore_signal(barrier, inc=1, device_id=peer, device_id_type=MESH)

    def greet_across():
        @pl.when(across)
        def _():
            greet(second)

        @pl.when(far_across)
        def _():
            greet(far)

    for peer in (x_dev, up, down, first, sibling):
        greet(peer)

    @pl.when(jnp.logical_not(across))
    def _():
        greet(second)

    @pl.when(jnp.logical_not(far_across))
    def _():
        greet(far)

    def block(ref, slot, start=0, size=rows):
        begin = slot * rows + start
        if not isinstance(begin, int):
            begin = pl.multiple_of(begin, rows)
        return ref.at[pl.ds(begin, size)]

    copies = {}

    def make(name, src, dst, device, lands=0):
        n = NUMBER[name]
        copies[name] = pltpu.make_async_remote_copy(
            src_ref=src, dst_ref=dst, send_sem=send_sem.at[n], recv_sem=recv_sem.at[n + lands],
            device_id=device, device_id_type=MESH,
        )
        return copies[name]

    def send(name, src, dst, device, lands=0):
        make(name, src, dst, device, lands).start()

    def arrived(*names):
        for name in names:
            copies[name].wait_recv()

    def came(name, dst):
        n = NUMBER[name]
        pltpu.make_async_remote_copy(
            src_ref=dst, dst_ref=dst, send_sem=send_sem.at[n], recv_sem=recv_sem.at[n],
            device_id=first, device_id_type=MESH,
        ).wait_recv()

    loads[0].wait()
    img[0:rows] = unit_of(pic)[0].astype(jnp.bfloat16)
    loads[1].wait()
    txt[0:rows] = unit_of(cap)[0].astype(jnp.bfloat16)
    sharp, shift = sharp_ref[0], shift_ref[0]

    pl.semaphore_wait(barrier, jnp.where(low, 7 - beyond, 7))
    greet_across()

    def half_of(ref, slot, n):
        return block(ref, slot, n * half, half)

    def move(name, n, ref, slot, dst, dst_slot, device):
        send(name, half_of(ref, slot, n), half_of(dst, dst_slot, n), device)

    move("x0", 0, img, 0, img, 1, x_dev)
    move("own+0", 0, img, 0, img, 3, up)
    move("own-1", 1, img, 0, img, 2, down)
    send("tsib", block(txt, 0), block(txt, 1), sibling)
    make("tsecond", block(txt, 0), block(txt, 2 + 2 * at_second), second, at_second - 1)
    make("tfar", block(txt, jnp.where(by_first, 2, 4)), block(txt, 6), far)

    @pl.when(jnp.logical_not(low & across))
    def _():
        copies["tsecond"].start()

    send("tfirst", block(txt, 0), block(txt, 2 + 2 * at_first), first, at_first)
    move("own+1", 1, img, 0, img, 3, up)
    move("own-0", 0, img, 0, img, 2, down)

    arrived("x0")
    move("x1", 1, img, 0, img, 1, x_dev)
    move("part+0", 0, img, 1, img, 5, up)
    move("part-0", 0, img, 1, img, 4, down)
    arrived("own+0", "own-1")
    move("fwd+", 0, img, 3, img, 6, up)
    move("fwd-", 1, img, 2, img, 6, down)

    arrived("x1")
    move("part-1", 1, img, 1, img, 4, down)
    move("part+1", 1, img, 1, img, 5, up)
    came("tfirst", block(txt, 2))
    send("tsib1", block(txt, 2), block(txt, 3), sibling)

    @pl.when(by_first & jnp.logical_not(low & far_across))
    def _():
        copies["tfar"].start()

    make("tsib2", block(txt, 4), block(txt, 5), sibling)

    def second_text():
        came("tsecond", block(txt, 4))
        copies["tsib2"].start()

        @pl.when(jnp.logical_not(by_first))
        def _():
            copies["tfar"].start()

    @pl.when(jnp.logical_not(across))
    def _():
        second_text()

    arrived("own+1", "own-0", "tsib", "tsib1")

    def score(slot, count, begin, end):
        here = pl.ds(slot * rows, count * rows)
        dots = lax.dot_general(
            img[here], txt[begin * rows : end * rows], (((1,), (1,)), ((), ())),
            preferred_element_type=jnp.float32,
        )
        chance = 1.0 / (1.0 + jnp.exp(-(sharp * dots + shift)))
        if slot == 0 and begin == 0:
            i = lax.broadcasted_iota(jnp.int32, chance.shape, 0)
            j = lax.broadcasted_iota(jnp.int32, chance.shape, 1)
            chance = chance - ((i == j) & (i < rows)).astype(jnp.float32)
        weights[here, begin * rows : end * rows] = (sharp * chance).astype(jnp.bfloat16)

    def image_grad(slot, count):
        here = pl.ds(slot * rows, count * rows)
        part[here] = jnp.dot(weights[here], txt[...], preferred_element_type=jnp.float32)

    def text_grad(begin, end):
        tgrad[begin * rows : end * rows] = lax.dot_general(
            weights[:, begin * rows : end * rows], img[...], (((0,), (0,)), ((), ())),
            preferred_element_type=jnp.float32,
        )

    def take(slot, start=0, size=rows):
        return part[slot * rows + start : slot * rows + start + size]

    def put(slot, value, start=0):
        begin = slot * rows + start
        isend[begin : begin + value.shape[0]] = value.astype(jnp.bfloat16)

    score(0, 4, 0, EARLY)
    arrived("part+0", "part-1")
    move("pfwd+", 0, img, 5, img, 7, up)
    move("pfwd-", 1, img, 4, img, 7, down)
    arrived("part+1", "part-0")
    score(4, 2, 0, EARLY)

    @pl.when(low & (beyond > 0))
    def _():
        pl.semaphore_wait(barrier, beyond)

        @pl.when(across)
        def _():
            copies["tsecond"].start()

        @pl.when(far_across)
        def _():
            copies["tfar"].start()

    @pl.when(across)
    def _():
        second_text()

    arrived("fwd+", "fwd-", "pfwd+", "pfwd-")
    score(6, 2, 0, EARLY)

    arrived("tsib2", "tfar")
    score(6, 2, EARLY, TEXTS)
    image_grad(6, 2)
    put(7, take(7))
    move("phalf+", 0, isend, 7, ihalf, 0, up)
    move("phalf-", 1, isend, 7, ihalf, 0, down)
    put(6, take(6))
    move("half+", 0, isend, 6, ihalf, 1, up)
    move("half-", 1, isend, 6, ihalf, 1, down)
    score(4, 2, EARLY, TEXTS)
    image_grad(4, 2)
    put(4, take(4, half, half), half)
    put(5, take(5, 0, half))
    move("pfull+1", 1, isend, 4, ifull, 0, up)
    move("pfull-0", 0, isend, 5, ifull, 1, down)
    score(0, 4, EARLY, TEXTS)

    def grad_rows(slot):
        return tgrad[slot * rows : (slot + 1) * rows]

    def put_text(n, value):
        tsend[n * rows : (n + 1) * rows] = value.astype(jnp.bfloat16)

    def got_text(n):
        return trecv[n * rows : (n + 1) * rows].astype(jnp.float32)

    text_grad(EARLY, TEXTS)
    put_text(6, grad_rows(6))
    send("gfar", block(tsend, 6), block(trecv, 5), far)
    put_text(5, grad_rows(5))
    send("gsib2", block(tsend, 5), block(trecv, 2), sibling)

    def got_half(n, start):
        begin = n * rows + start
        return ihalf[begin : begin + half].astype(jnp.float32)

    arrived("phalf+", "phalf-")
    put(4, take(4, 0, half) + got_half(0, 0))
    put(5, take(5, half, half) + got_half(0, half), half)
    move("pfull+0", 0, isend, 4, ifull, 0, up)
    move("pfull-1", 1, isend, 5, ifull, 1, down)

    image_grad(0, 4)
    put(2, take(2, half, half), half)
    put(3, take(3, 0, half))
    move("full+1", 1, isend, 2, ifull, 2, up)
    move("full-0", 0, isend, 3, ifull, 3, down)

    text_grad(0, EARLY)
    put_text(3, grad_rows(3))
    send("gsib1", block(tsend, 3), block(trecv, 1), sibling)
    put_text(1, grad_rows(1))
    send("gsib", block(tsend, 1), block(trecv, 0), sibling)

    arrived("half+", "half-")
    put(2, take(2, 0, half) + got_half(1, 0))
    put(3, take(3, half, half) + got_half(1, half), half)
    move("full+0", 0, isend, 2, ifull, 2, up)
    move("full-1", 1, isend, 3, ifull, 3, down)

    arrived("gsib2")

    def send_second(extra):
        put_text(4, grad_rows(4) + got_text(2) + extra)
        send("gsecond", block(tsend, 4), block(trecv, 3 + at_second), second, at_second - 1)

    def send_first(extra):
        put_text(2, grad_rows(2) + got_text(1) + extra)
        send("gfirst", block(tsend, 2), block(trecv, 3 + at_first), first, at_first)

    arrived("gsib1", "gfar")
    send_second(jnp.where(by_first, 0.0, got_text(5)))
    send_first(jnp.where(by_first, got_text(5), 0.0))

    def got_full(n):
        return ifull[n * rows : (n + 1) * rows].astype(jnp.float32)

    arrived("pfull+0", "pfull+1", "pfull-0", "pfull-1")
    put(1, take(1) + got_full(0) + got_full(1))
    send("xsum", block(isend, 1), block(ifull, 4), x_dev)

    arrived("gsib")
    came("gfirst", block(trecv, 3))
    came("gsecond", block(trecv, 4))
    def back(ref, grad):
        unit, inverse = unit_of(ref)
        return inverse * (grad - unit * jnp.sum(unit * grad, axis=-1, keepdims=True))

    cap_hat_grad = grad_rows(0) + got_text(0) + got_text(3) + got_text(4)
    cap_out[...] = back(cap, cap_hat_grad)

    arrived("full+0", "full+1", "full-0", "full-1", "xsum")
    pic_out[...] = back(pic, take(0) + got_full(2) + got_full(3) + got_full(4))

    for name in COPIES:
        copies[name].wait_send()


def shards(picture_embedding_raw, caption_embedding_raw, score_sharpness, score_shift_term):
    rows, width = picture_embedding_raw.shape
    n_pool = lax.axis_size("pool")
    result = jax.ShapeDtypeStruct((rows, width), jnp.float32)

    def blocks(count, dtype=jnp.bfloat16):
        return pltpu.VMEM((count * rows, width), dtype)

    vmem = pl.BlockSpec(memory_space=pltpu.VMEM)
    smem = pl.BlockSpec(memory_space=pltpu.SMEM)
    hbm = pl.BlockSpec(memory_space=pltpu.HBM)
    return pl.pallas_call(
        kernel,
        out_shape=(result, result),
        in_specs=[smem, smem, hbm, hbm],
        out_specs=(vmem, vmem),
        scratch_shapes=[
            blocks(1),
            blocks(1),
            blocks(n_pool),
            blocks(TEXTS),
            pltpu.VMEM((n_pool * rows, TEXTS * rows), jnp.bfloat16),
            blocks(n_pool, jnp.float32),
            blocks(TEXTS, jnp.float32),
            blocks(n_pool),
            blocks(2),
            blocks(5),
            blocks(TEXTS),
            blocks(6),
            pltpu.SemaphoreType.DMA((len(COPIES),)),
            pltpu.SemaphoreType.DMA((len(COPIES),)),
            pltpu.SemaphoreType.DMA((2,)),
        ],
        compiler_params=pltpu.CompilerParams(
            collective_id=0, has_side_effects=True, vmem_limit_bytes=40 * 2**20
        ),
    )(score_sharpness, score_shift_term, picture_embedding_raw, caption_embedding_raw)

def solution(mesh):
    return jax.shard_map(
        shards,
        mesh=mesh,
        in_specs=(P(("loop", "pool"), None), P(("loop", "pool"), None), P(), P()),
        out_specs=(P(("loop", "pool"), None), P(("loop", "pool"), None)),
        check_vma=False,
    )
```

```python
import jax
import jax.numpy as jnp
from jax import lax
from jax.experimental import pallas as pl
from jax.experimental.pallas import tpu as pltpu
from jax.sharding import PartitionSpec as P

MESH = pl.DeviceIdType.MESH
epsilon_norm = 1e-06

TEXTS = 7
EARLY = 4

QUARTERS = 4
PARTS = {"A": (0, 2), "B": (2, 2), "A0": (0, 1), "A1": (1, 1), "B0": (2, 1), "B1": (3, 1)}

COPIES = (
    "xA", "xB0", "xB2", "xB3", "xB6", "ownA+", "ownA-", "ownB+", "ownB-", "partA+", "partA-",
    "fwdA+", "fwdA-", "fwdB+", "fwdB-", "pfwdA+", "pfwdA-",
    "tsib", "tfirst", "tsecond", "tfar", "tsib1", "tsib2",
    "xsum7", "xsum4", "xsum5", "xsum1", "xsumA", "phalfA+", "phalfA-", "halfA+", "halfA-", "halfB+", "halfB-",
    "pfullA+0", "pfullA+1", "pfullA-0", "pfullA-1", "fullA+0", "fullA+1", "fullA-0", "fullA-1",
    "fullB+", "fullB-",
    "gsib", "gsib1", "gsib2", "gfirst", "gsecond", "gfar",
)
NUMBER = {name: i for i, name in enumerate(COPIES)}


def inverse_norm(wide):
    return lax.rsqrt(jnp.sum(wide * wide, axis=-1, keepdims=True) + epsilon_norm)


def unit_of(ref):
    wide = ref[...].astype(jnp.float32)
    inverse = inverse_norm(wide)
    return wide * inverse, inverse


def kernel(
    sharp_ref, shift_ref, pic_ref, cap_ref, pic_out, cap_out,
    pic, cap, img, txt, weights, part_sum, tgrad, isend, ixsum, ihalf, ifull, tsend, trecv,
    send_sem, recv_sem, load_sem,
):
    rows, width = pic_ref.shape
    loads = [
        pltpu.make_async_copy(ref, dst, load_sem.at[n])
        for n, (ref, dst) in enumerate(((pic_ref, pic), (cap_ref, cap)))
    ]
    for load in loads:
        load.start()
    quarter = rows // QUARTERS
    n_loop = lax.axis_size("loop")
    n_z = n_loop // 4
    group, cls = lax.axis_index("loop"), lax.axis_index("pool")
    sign = 1 - 2 * lax.rem(group, 2)
    z = lax.rem(group // 2, n_z)
    n_y = lax.axis_size("pool") // 2
    x, y = cls // n_y, lax.rem(cls, n_y)
    x_dev = (group, (1 - x) * n_y + y)
    up = (group, x * n_y + lax.rem(y + 1, n_y))
    down = (group, x * n_y + lax.rem(y + n_y - 1, n_y))
    toward = jnp.where(z == n_z - 1, -2, 2)
    first = (lax.rem(group + n_loop + toward, n_loop), cls)
    at_first = jnp.where(z >= n_z - 2, 0, 1)
    across = (z == 0) | (z == n_z - 1)
    at_second = jnp.where(across, 1, 0)
    sibling = (group + sign, cls)
    far_across = jnp.where(sign > 0, z == 0, z == n_z - 1)
    by_first = sign * 2 == toward
    mirror = (1 - x) * n_y + y
    second = (lax.rem(group + n_loop - toward, n_loop), jnp.where(across, mirror, cls))
    far = (lax.rem(group + n_loop - sign, n_loop), jnp.where(far_across, mirror, cls))
    low = z == 0
    beyond = across.astype(jnp.int32) + far_across.astype(jnp.int32)

    barrier = pltpu.get_barrier_semaphore()

    def greet(peer):
        pl.semaphore_signal(barrier, inc=1, device_id=peer, device_id_type=MESH)

    def greet_across():
        @pl.when(across)
        def _():
            greet(second)

        @pl.when(far_across)
        def _():
            greet(far)

    for peer in (x_dev, up, down, first, sibling):
        greet(peer)

    @pl.when(jnp.logical_not(across))
    def _():
        greet(second)

    @pl.when(jnp.logical_not(far_across))
    def _():
        greet(far)

    def block(ref, slot, start=0, size=rows):
        begin = slot * rows + start
        if not isinstance(begin, int):
            begin = pl.multiple_of(begin, rows)
        return ref.at[pl.ds(begin, size)]

    copies = {}

    def make(name, src, dst, device, lands=0):
        n = NUMBER[name]
        copies[name] = pltpu.make_async_remote_copy(
            src_ref=src, dst_ref=dst, send_sem=send_sem.at[n], recv_sem=recv_sem.at[n + lands],
            device_id=device, device_id_type=MESH,
        )
        return copies[name]

    def send(name, src, dst, device, lands=0):
        make(name, src, dst, device, lands).start()

    def arrived(*names):
        for name in names:
            copies[name].wait_recv()

    def came(name, dst):
        n = NUMBER[name]
        pltpu.make_async_remote_copy(
            src_ref=dst, dst_ref=dst, send_sem=send_sem.at[n], recv_sem=recv_sem.at[n],
            device_id=first, device_id_type=MESH,
        ).wait_recv()

    loads[0].wait()
    img[0:rows] = unit_of(pic)[0].astype(jnp.bfloat16)
    loads[1].wait()
    txt[0:rows] = unit_of(cap)[0].astype(jnp.bfloat16)
    sharp, shift = sharp_ref[0], shift_ref[0]

    pl.semaphore_wait(barrier, jnp.where(low, 7 - beyond, 7))
    greet_across()

    def place(part):
        first_quarter, count = PARTS[part]
        return first_quarter * quarter, count * quarter

    def piece(ref, slot, part):
        return block(ref, slot, *place(part))

    def move(name, part, ref, slot, dst, dst_slot, device):
        send(name, piece(ref, slot, part), piece(dst, dst_slot, part), device)

    move("xA", "A", img, 0, img, 1, x_dev)
    move("ownB+", "B", img, 0, img, 3, up)
    move("ownB-", "B", img, 0, img, 2, down)
    send("tsib", block(txt, 0), block(txt, 1), sibling)
    make("tsecond", block(txt, 0), block(txt, 2 + 2 * at_second), second, at_second - 1)
    make("tfar", block(txt, jnp.where(by_first, 2, 4)), block(txt, 6), far)

    @pl.when(jnp.logical_not(low & across))
    def _():
        copies["tsecond"].start()

    send("tfirst", block(txt, 0), block(txt, 2 + 2 * at_first), first, at_first)
    move("ownA+", "A", img, 0, img, 3, up)
    move("ownA-", "A", img, 0, img, 2, down)
    move("xB0", "B", img, 0, img, 1, x_dev)

    arrived("ownB+", "ownB-")
    move("fwdB+", "B0", img, 3, img, 6, up)
    move("fwdB-", "B1", img, 2, img, 6, down)
    move("xB2", "B", img, 2, img, 4, x_dev)
    move("xB3", "B", img, 3, img, 5, x_dev)
    arrived("xA")
    move("partA+", "A", img, 1, img, 5, up)
    move("partA-", "A", img, 1, img, 4, down)
    arrived("ownA+", "ownA-")
    move("fwdA+", "A0", img, 3, img, 6, up)
    move("fwdA-", "A1", img, 2, img, 6, down)
    came("tfirst", block(txt, 2))
    send("tsib1", block(txt, 2), block(txt, 3), sibling)

    @pl.when(by_first & jnp.logical_not(low & far_across))
    def _():
        copies["tfar"].start()

    arrived("fwdB+", "fwdB-")
    move("xB6", "B", img, 6, img, 7, x_dev)
    make("tsib2", block(txt, 4), block(txt, 5), sibling)

    def second_text():
        came("tsecond", block(txt, 4))
        copies["tsib2"].start()

        @pl.when(jnp.logical_not(by_first))
        def _():
            copies["tfar"].start()

    @pl.when(jnp.logical_not(across))
    def _():
        second_text()

    arrived("xB0", "tsib", "tsib1")

    def score(slot, count, begin, end):
        here = pl.ds(slot * rows, count * rows)
        dots = lax.dot_general(
            img[here], txt[begin * rows : end * rows], (((1,), (1,)), ((), ())),
            preferred_element_type=jnp.float32,
        )
        chance = 1.0 / (1.0 + jnp.exp(-(sharp * dots + shift)))
        if slot == 0 and begin == 0:
            i = lax.broadcasted_iota(jnp.int32, chance.shape, 0)
            j = lax.broadcasted_iota(jnp.int32, chance.shape, 1)
            chance = chance - ((i == j) & (i < rows)).astype(jnp.float32)
        weights[here, begin * rows : end * rows] = (sharp * chance).astype(jnp.bfloat16)

    def image_grad(slot, count):
        here = pl.ds(slot * rows, count * rows)
        part_sum[here] = jnp.dot(weights[here], txt[...], preferred_element_type=jnp.float32)

    def text_grad(begin, end):
        tgrad[begin * rows : end * rows] = lax.dot_general(
            weights[:, begin * rows : end * rows], img[...], (((0,), (0,)), ((), ())),
            preferred_element_type=jnp.float32,
        )

    def take(slot, part):
        start, size = place(part)
        return part_rows(part_sum, slot, start, size)

    def part_rows(ref, slot, start, size):
        return ref[slot * rows + start : slot * rows + start + size]

    def put(slot, part, *extra):
        start, size = place(part)
        value = take(slot, part)
        for ref, ref_slot in extra:
            value = value + part_rows(ref, ref_slot, start, size).astype(jnp.float32)
        isend[slot * rows + start : slot * rows + start + size] = value.astype(jnp.bfloat16)

    score(0, 4, 0, EARLY)
    arrived("partA+", "partA-")
    move("pfwdA+", "A0", img, 5, img, 7, up)
    move("pfwdA-", "A1", img, 4, img, 7, down)

    @pl.when(low & (beyond > 0))
    def _():
        pl.semaphore_wait(barrier, beyond)

        @pl.when(across)
        def _():
            copies["tsecond"].start()

        @pl.when(far_across)
        def _():
            copies["tfar"].start()

    arrived("xB2", "xB3")
    score(4, 2, 0, EARLY)

    @pl.when(across)
    def _():
        second_text()

    arrived("fwdA+", "fwdA-", "pfwdA+", "pfwdA-", "xB6")
    score(6, 2, 0, EARLY)

    arrived("tsib2", "tfar")
    score(6, 2, EARLY, TEXTS)
    image_grad(6, 2)
    put(7, "B")
    move("xsum7", "B", isend, 7, ixsum, 3, x_dev)
    put(7, "A")
    move("phalfA+", "A0", isend, 7, ihalf, 0, up)
    move("phalfA-", "A1", isend, 7, ihalf, 0, down)
    put(6, "A")
    move("halfA+", "A0", isend, 6, ihalf, 1, up)
    move("halfA-", "A1", isend, 6, ihalf, 1, down)
    score(4, 2, EARLY, TEXTS)
    image_grad(4, 2)
    put(4, "B")
    move("xsum4", "B", isend, 4, ixsum, 1, x_dev)
    put(5, "B")
    move("xsum5", "B", isend, 5, ixsum, 2, x_dev)
    put(4, "A1")
    move("pfullA+1", "A1", isend, 4, ifull, 0, up)
    put(5, "A0")
    move("pfullA-0", "A0", isend, 5, ifull, 1, down)
    score(0, 4, EARLY, TEXTS)
    arrived("xsum7")
    put(6, "B", (ixsum, 3))
    move("halfB+", "B0", isend, 6, ihalf, 1, up)
    move("halfB-", "B1", isend, 6, ihalf, 1, down)

    def grad_rows(slot):
        return tgrad[slot * rows : (slot + 1) * rows]

    def put_text(n, value):
        tsend[n * rows : (n + 1) * rows] = value.astype(jnp.bfloat16)

    def got_text(n):
        return trecv[n * rows : (n + 1) * rows].astype(jnp.float32)

    text_grad(EARLY, TEXTS)
    put_text(6, grad_rows(6))
    send("gfar", block(tsend, 6), block(trecv, 5), far)
    put_text(5, grad_rows(5))
    send("gsib2", block(tsend, 5), block(trecv, 2), sibling)

    arrived("phalfA+", "phalfA-")
    put(4, "A0", (ihalf, 0))
    move("pfullA+0", "A0", isend, 4, ifull, 0, up)
    put(5, "A1", (ihalf, 0))
    move("pfullA-1", "A1", isend, 5, ifull, 1, down)

    image_grad(0, 4)
    put(1, "B")
    move("xsum1", "B", isend, 1, ixsum, 0, x_dev)
    put(2, "A1")
    move("fullA+1", "A1", isend, 2, ifull, 2, up)
    put(3, "A0")
    move("fullA-0", "A0", isend, 3, ifull, 3, down)

    arrived("halfA+", "halfA-")
    put(2, "A0", (ihalf, 1))
    move("fullA+0", "A0", isend, 2, ifull, 2, up)
    put(3, "A1", (ihalf, 1))
    move("fullA-1", "A1", isend, 3, ifull, 3, down)

    text_grad(0, EARLY)
    put_text(3, grad_rows(3))
    send("gsib1", block(tsend, 3), block(trecv, 1), sibling)
    put_text(1, grad_rows(1))
    send("gsib", block(tsend, 1), block(trecv, 0), sibling)

    arrived("pfullA+0", "pfullA+1", "pfullA-0", "pfullA-1")
    put(1, "A", (ifull, 0), (ifull, 1))
    move("xsumA", "A", isend, 1, ifull, 4, x_dev)

    arrived("xsum4", "xsum5", "halfB+", "halfB-")
    put(2, "B0", (ixsum, 1), (ihalf, 1))
    put(2, "B1", (ixsum, 1))
    move("fullB+", "B", isend, 2, ifull, 2, up)
    put(3, "B0", (ixsum, 2))
    put(3, "B1", (ixsum, 2), (ihalf, 1))
    move("fullB-", "B", isend, 3, ifull, 3, down)

    def text_rows(ref, slot):
        return ref[pl.ds(pl.multiple_of(slot * rows, rows), rows)].astype(jnp.float32)

    def pass_back(name, is_first, *parts):
        slot = jnp.where(is_first, 2, 4)
        value = text_rows(tgrad, slot) + text_rows(trecv, jnp.where(is_first, 1, 2))
        for n in parts:
            value = value + got_text(n)
        tsend[pl.ds(pl.multiple_of(slot * rows, rows), rows)] = value.astype(jnp.bfloat16)
        lands = jnp.where(is_first, at_first, at_second)
        device = tuple(jnp.where(is_first, a, b) for a, b in zip(first, second))
        send(name, block(tsend, slot), block(trecv, 3 + lands), device, lands - (name == "gsecond"))

    arrived("gsib1", "gsib2")
    pass_back("gfirst", jnp.logical_not(by_first))
    arrived("gfar")
    pass_back("gsecond", by_first, 5)

    def got_full(n):
        return ifull[n * rows : (n + 1) * rows].astype(jnp.float32)

    arrived("gsib")
    came("gfirst", block(trecv, 3))
    came("gsecond", block(trecv, 4))
    def back(ref, grad):
        unit, inverse = unit_of(ref)
        return inverse * (grad - unit * jnp.sum(unit * grad, axis=-1, keepdims=True))

    cap_hat_grad = grad_rows(0) + got_text(0) + got_text(3) + got_text(4)
    cap_out[...] = back(cap, cap_hat_grad)

    arrived("fullA+0", "fullA+1", "fullA-0", "fullA-1", "xsumA", "xsum1", "fullB+", "fullB-")
    size = place("A")[1]
    crossed = (got_full(4)[:size], ixsum[size : 2 * size].astype(jnp.float32))
    pic_hat_grad = part_sum[0:rows] + got_full(2) + got_full(3) + jnp.concatenate(crossed, axis=0)
    pic_out[...] = back(pic, pic_hat_grad)

    for name in COPIES:
        copies[name].wait_send()


def shards(picture_embedding_raw, caption_embedding_raw, score_sharpness, score_shift_term):
    rows, width = picture_embedding_raw.shape
    n_pool = lax.axis_size("pool")
    result = jax.ShapeDtypeStruct((rows, width), jnp.float32)

    def blocks(count, dtype=jnp.bfloat16):
        return pltpu.VMEM((count * rows, width), dtype)

    vmem = pl.BlockSpec(memory_space=pltpu.VMEM)
    smem = pl.BlockSpec(memory_space=pltpu.SMEM)
    hbm = pl.BlockSpec(memory_space=pltpu.HBM)
    return pl.pallas_call(
        kernel,
        out_shape=(result, result),
        in_specs=[smem, smem, hbm, hbm],
        out_specs=(vmem, vmem),
        scratch_shapes=[
            blocks(1),
            blocks(1),
            blocks(n_pool),
            blocks(TEXTS),
            pltpu.VMEM((n_pool * rows, TEXTS * rows), jnp.bfloat16),
            blocks(n_pool, jnp.float32),
            blocks(TEXTS, jnp.float32),
            blocks(n_pool),
            blocks(4),
            blocks(2),
            blocks(5),
            blocks(TEXTS),
            blocks(6),
            pltpu.SemaphoreType.DMA((len(COPIES),)),
            pltpu.SemaphoreType.DMA((len(COPIES),)),
            pltpu.SemaphoreType.DMA((2,)),
        ],
        compiler_params=pltpu.CompilerParams(
            collective_id=0, has_side_effects=True, vmem_limit_bytes=40 * 2**20
        ),
    )(score_sharpness, score_shift_term, picture_embedding_raw, caption_embedding_raw)

def solution(mesh):
    return jax.shard_map(
        shards,
        mesh=mesh,
        in_specs=(P(("loop", "pool"), None), P(("loop", "pool"), None), P(), P()),
        out_specs=(P(("loop", "pool"), None), P(("loop", "pool"), None)),
        check_vma=False,
    )
```

```python
import jax
import jax.numpy as jnp
from jax import lax
from jax.experimental import pallas as pl
from jax.experimental.pallas import tpu as pltpu
from jax.sharding import PartitionSpec as P

MESH = pl.DeviceIdType.MESH
epsilon_norm = 1e-06

TEXTS = 7
EARLY = 4

QUARTERS = 4
PARTS = {"A": (0, 2), "B": (2, 2), "A0": (0, 1), "A1": (1, 1), "B0": (2, 1), "B1": (3, 1)}

COPIES = (
    "xA", "xB0", "xB2", "xB3", "xB6", "ownA+", "ownA-", "ownB+", "ownB-", "partA+", "partA-",
    "fwdA+", "fwdA-", "fwdB+", "fwdB-", "pfwdA+", "pfwdA-",
    "tsib", "tfirst", "tsecond", "tfar", "tsib1", "tsib2",
    "xsum7", "xsum4", "xsum5", "xsum1", "xsumA", "phalfA+", "phalfA-", "halfA+", "halfA-", "halfB+", "halfB-",
    "pfullA+0", "pfullA+1", "pfullA-0", "pfullA-1", "fullA+0", "fullA+1", "fullA-0", "fullA-1",
    "fullB+", "fullB-",
    "gsib", "gsib1", "gsib2", "gfirst", "gsecond", "gfar",
)
NUMBER = {name: i for i, name in enumerate(COPIES)}


def inverse_norm(wide):
    return lax.rsqrt(jnp.sum(wide * wide, axis=-1, keepdims=True) + epsilon_norm)


def unit_of(ref):
    wide = ref[...].astype(jnp.float32)
    inverse = inverse_norm(wide)
    return wide * inverse, inverse


def kernel(
    sharp_ref, shift_ref, pic, cap, pic_out, cap_out,
    img, txt, weights, part_sum, tgrad, isend, ixsum, ihalf, ifull, tsend, trecv,
    send_sem, recv_sem,
):
    rows, width = pic.shape
    quarter = rows // QUARTERS
    n_loop = lax.axis_size("loop")
    n_z = n_loop // 4
    group, cls = lax.axis_index("loop"), lax.axis_index("pool")
    sign = 1 - 2 * lax.rem(group, 2)
    z = lax.rem(group // 2, n_z)
    n_y = lax.axis_size("pool") // 2
    x, y = cls // n_y, lax.rem(cls, n_y)
    x_dev = (group, (1 - x) * n_y + y)
    up = (group, x * n_y + lax.rem(y + 1, n_y))
    down = (group, x * n_y + lax.rem(y + n_y - 1, n_y))
    toward = jnp.where(z == n_z - 1, -2, 2)
    first = (lax.rem(group + n_loop + toward, n_loop), cls)
    at_first = jnp.where(z >= n_z - 2, 0, 1)
    across = (z == 0) | (z == n_z - 1)
    at_second = jnp.where(across, 1, 0)
    sibling = (group + sign, cls)
    far_across = jnp.where(sign > 0, z == 0, z == n_z - 1)
    by_first = sign * 2 == toward
    mirror = (1 - x) * n_y + y
    second = (lax.rem(group + n_loop - toward, n_loop), jnp.where(across, mirror, cls))
    far = (lax.rem(group + n_loop - sign, n_loop), jnp.where(far_across, mirror, cls))
    low = z == 0
    beyond = across.astype(jnp.int32) + far_across.astype(jnp.int32)

    barrier = pltpu.get_barrier_semaphore()

    def greet(peer):
        pl.semaphore_signal(barrier, inc=1, device_id=peer, device_id_type=MESH)

    def greet_across():
        @pl.when(across)
        def _():
            greet(second)

        @pl.when(far_across)
        def _():
            greet(far)

    for peer in (x_dev, up, down, first, sibling):
        greet(peer)

    @pl.when(jnp.logical_not(across))
    def _():
        greet(second)

    @pl.when(jnp.logical_not(far_across))
    def _():
        greet(far)

    def block(ref, slot, start=0, size=rows):
        begin = slot * rows + start
        if not isinstance(begin, int):
            begin = pl.multiple_of(begin, rows)
        return ref.at[pl.ds(begin, size)]

    copies = {}

    def make(name, src, dst, device, lands=0):
        n = NUMBER[name]
        copies[name] = pltpu.make_async_remote_copy(
            src_ref=src, dst_ref=dst, send_sem=send_sem.at[n], recv_sem=recv_sem.at[n + lands],
            device_id=device, device_id_type=MESH,
        )
        return copies[name]

    def send(name, src, dst, device, lands=0):
        make(name, src, dst, device, lands).start()

    def arrived(*names):
        for name in names:
            copies[name].wait_recv()

    def came(name, dst):
        n = NUMBER[name]
        pltpu.make_async_remote_copy(
            src_ref=dst, dst_ref=dst, send_sem=send_sem.at[n], recv_sem=recv_sem.at[n],
            device_id=first, device_id_type=MESH,
        ).wait_recv()

    img[0:rows] = unit_of(pic)[0].astype(jnp.bfloat16)
    txt[0:rows] = unit_of(cap)[0].astype(jnp.bfloat16)
    sharp, shift = sharp_ref[0], shift_ref[0]

    pl.semaphore_wait(barrier, jnp.where(low, 7 - beyond, 7))
    greet_across()

    def place(part):
        first_quarter, count = PARTS[part]
        return first_quarter * quarter, count * quarter

    def piece(ref, slot, part):
        return block(ref, slot, *place(part))

    def move(name, part, ref, slot, dst, dst_slot, device):
        send(name, piece(ref, slot, part), piece(dst, dst_slot, part), device)

    move("xA", "A", img, 0, img, 1, x_dev)
    move("ownB+", "B", img, 0, img, 3, up)
    move("ownB-", "B", img, 0, img, 2, down)
    send("tsib", block(txt, 0), block(txt, 1), sibling)
    make("tsecond", block(txt, 0), block(txt, 2 + 2 * at_second), second, at_second - 1)
    make("tfar", block(txt, jnp.where(by_first, 2, 4)), block(txt, 6), far)

    @pl.when(jnp.logical_not(low & across))
    def _():
        copies["tsecond"].start()

    send("tfirst", block(txt, 0), block(txt, 2 + 2 * at_first), first, at_first)
    move("ownA+", "A", img, 0, img, 3, up)
    move("ownA-", "A", img, 0, img, 2, down)
    move("xB0", "B", img, 0, img, 1, x_dev)

    arrived("ownB+", "ownB-")
    move("fwdB+", "B0", img, 3, img, 6, up)
    move("fwdB-", "B1", img, 2, img, 6, down)
    move("xB2", "B", img, 2, img, 4, x_dev)
    move("xB3", "B", img, 3, img, 5, x_dev)
    arrived("xA")
    move("partA+", "A", img, 1, img, 5, up)
    move("partA-", "A", img, 1, img, 4, down)
    arrived("ownA+", "ownA-")
    move("fwdA+", "A0", img, 3, img, 6, up)
    move("fwdA-", "A1", img, 2, img, 6, down)
    came("tfirst", block(txt, 2))
    send("tsib1", block(txt, 2), block(txt, 3), sibling)

    @pl.when(by_first & jnp.logical_not(low & far_across))
    def _():
        copies["tfar"].start()

    arrived("fwdB+", "fwdB-")
    move("xB6", "B", img, 6, img, 7, x_dev)
    make("tsib2", block(txt, 4), block(txt, 5), sibling)

    def second_text():
        came("tsecond", block(txt, 4))
        copies["tsib2"].start()

        @pl.when(jnp.logical_not(by_first))
        def _():
            copies["tfar"].start()

    @pl.when(jnp.logical_not(across))
    def _():
        second_text()

    arrived("xB0", "tsib", "tsib1")

    def score(slot, count, begin, end):
        here = pl.ds(slot * rows, count * rows)
        dots = lax.dot_general(
            img[here], txt[begin * rows : end * rows], (((1,), (1,)), ((), ())),
            preferred_element_type=jnp.float32,
        )
        chance = 1.0 / (1.0 + jnp.exp(-(sharp * dots + shift)))
        if slot == 0 and begin == 0:
            i = lax.broadcasted_iota(jnp.int32, chance.shape, 0)
            j = lax.broadcasted_iota(jnp.int32, chance.shape, 1)
            chance = chance - ((i == j) & (i < rows)).astype(jnp.float32)
        weights[here, begin * rows : end * rows] = (sharp * chance).astype(jnp.bfloat16)

    def image_grad(slot, count):
        here = pl.ds(slot * rows, count * rows)
        part_sum[here] = jnp.dot(weights[here], txt[...], preferred_element_type=jnp.float32)

    def text_grad(begin, end):
        tgrad[begin * rows : end * rows] = lax.dot_general(
            weights[:, begin * rows : end * rows], img[...], (((0,), (0,)), ((), ())),
            preferred_element_type=jnp.float32,
        )

    def take(slot, part):
        start, size = place(part)
        return part_rows(part_sum, slot, start, size)

    def part_rows(ref, slot, start, size):
        return ref[slot * rows + start : slot * rows + start + size]

    def put(slot, part, *extra):
        start, size = place(part)
        value = take(slot, part)
        for ref, ref_slot in extra:
            value = value + part_rows(ref, ref_slot, start, size).astype(jnp.float32)
        isend[slot * rows + start : slot * rows + start + size] = value.astype(jnp.bfloat16)

    score(0, 4, 0, EARLY)

    @pl.when(low & (beyond > 0))
    def _():
        pl.semaphore_wait(barrier, beyond)

        @pl.when(across)
        def _():
            copies["tsecond"].start()

        @pl.when(far_across)
        def _():
            copies["tfar"].start()

    arrived("partA+", "partA-")
    move("pfwdA+", "A0", img, 5, img, 7, up)
    move("pfwdA-", "A1", img, 4, img, 7, down)

    arrived("xB2", "xB3")
    score(4, 2, 0, EARLY)

    @pl.when(across)
    def _():
        second_text()

    arrived("fwdA+", "fwdA-", "pfwdA+", "pfwdA-", "xB6")
    score(6, 2, 0, EARLY)

    arrived("tsib2", "tfar")
    score(6, 2, EARLY, TEXTS)
    image_grad(6, 2)
    put(7, "B")
    move("xsum7", "B", isend, 7, ixsum, 3, x_dev)
    put(7, "A")
    move("phalfA+", "A0", isend, 7, ihalf, 0, up)
    move("phalfA-", "A1", isend, 7, ihalf, 0, down)
    put(6, "A")
    move("halfA+", "A0", isend, 6, ihalf, 1, up)
    move("halfA-", "A1", isend, 6, ihalf, 1, down)
    score(4, 2, EARLY, TEXTS)
    image_grad(4, 2)
    put(4, "B")
    move("xsum4", "B", isend, 4, ixsum, 1, x_dev)
    put(5, "B")
    move("xsum5", "B", isend, 5, ixsum, 2, x_dev)
    put(4, "A1")
    move("pfullA+1", "A1", isend, 4, ifull, 0, up)
    put(5, "A0")
    move("pfullA-0", "A0", isend, 5, ifull, 1, down)
    score(0, 4, EARLY, TEXTS)

    def grad_rows(slot):
        return tgrad[slot * rows : (slot + 1) * rows]

    def put_text(n, value):
        tsend[n * rows : (n + 1) * rows] = value.astype(jnp.bfloat16)

    def got_text(n):
        return trecv[n * rows : (n + 1) * rows].astype(jnp.float32)

    text_grad(EARLY, TEXTS)
    put_text(6, grad_rows(6))
    send("gfar", block(tsend, 6), block(trecv, 5), far)
    put_text(5, grad_rows(5))
    send("gsib2", block(tsend, 5), block(trecv, 2), sibling)

    arrived("phalfA+", "phalfA-")
    put(4, "A0", (ihalf, 0))
    move("pfullA+0", "A0", isend, 4, ifull, 0, up)
    put(5, "A1", (ihalf, 0))
    move("pfullA-1", "A1", isend, 5, ifull, 1, down)

    image_grad(0, 4)
    put(1, "B")
    move("xsum1", "B", isend, 1, ixsum, 0, x_dev)
    put(2, "A1")
    move("fullA+1", "A1", isend, 2, ifull, 2, up)
    put(3, "A0")
    move("fullA-0", "A0", isend, 3, ifull, 3, down)
    arrived("halfA+", "halfA-")
    put(2, "A0", (ihalf, 1))
    move("fullA+0", "A0", isend, 2, ifull, 2, up)
    put(3, "A1", (ihalf, 1))
    move("fullA-1", "A1", isend, 3, ifull, 3, down)

    arrived("xsum7")
    put(6, "B", (ixsum, 3))
    move("halfB+", "B0", isend, 6, ihalf, 1, up)
    move("halfB-", "B1", isend, 6, ihalf, 1, down)

    text_grad(0, EARLY)
    put_text(3, grad_rows(3))
    send("gsib1", block(tsend, 3), block(trecv, 1), sibling)
    put_text(1, grad_rows(1))
    send("gsib", block(tsend, 1), block(trecv, 0), sibling)

    def pass_back(name, slot, other, more):
        @pl.when(more)
        def _():
            arrived("gfar")
            put_text(slot, grad_rows(slot) + got_text(other) + got_text(5))

        @pl.when(jnp.logical_not(more))
        def _():
            put_text(slot, grad_rows(slot) + got_text(other))

        copies[name].start()

    make("gfirst", block(tsend, 2), block(trecv, 3 + at_first), first, at_first)
    make("gsecond", block(tsend, 4), block(trecv, 3 + at_second), second, at_second - 1)

    arrived("gsib2")
    pass_back("gsecond", 4, 2, jnp.logical_not(by_first))

    arrived("pfullA+0", "pfullA+1", "pfullA-0", "pfullA-1")
    put(1, "A", (ifull, 0), (ifull, 1))
    move("xsumA", "A", isend, 1, ifull, 4, x_dev)

    arrived("gsib1")

    def pass_first():
        pass_back("gfirst", 2, 1, by_first)

    @pl.when(jnp.logical_not(low & far_across))
    def _():
        pass_first()

    arrived("xsum4", "xsum5", "halfB+", "halfB-")
    put(2, "B0", (ixsum, 1), (ihalf, 1))
    put(2, "B1", (ixsum, 1))
    move("fullB+", "B", isend, 2, ifull, 2, up)
    put(3, "B0", (ixsum, 2))
    put(3, "B1", (ixsum, 2), (ihalf, 1))
    move("fullB-", "B", isend, 3, ifull, 3, down)

    @pl.when(low & far_across)
    def _():
        pass_first()

    def got_full(n):
        return ifull[n * rows : (n + 1) * rows].astype(jnp.float32)

    arrived("gsib")
    came("gfirst", block(trecv, 3))
    came("gsecond", block(trecv, 4))
    def back(ref, grad):
        unit, inverse = unit_of(ref)
        return inverse * (grad - unit * jnp.sum(unit * grad, axis=-1, keepdims=True))

    cap_hat_grad = grad_rows(0) + got_text(0) + got_text(3) + got_text(4)
    cap_out[...] = back(cap, cap_hat_grad)

    arrived("fullA+0", "fullA+1", "fullA-0", "fullA-1", "xsumA", "xsum1", "fullB+", "fullB-")
    size = place("A")[1]
    crossed = (got_full(4)[:size], ixsum[size : 2 * size].astype(jnp.float32))
    pic_hat_grad = part_sum[0:rows] + got_full(2) + got_full(3) + jnp.concatenate(crossed, axis=0)
    pic_out[...] = back(pic, pic_hat_grad)

    for name in COPIES:
        copies[name].wait_send()


def shards(picture_embedding_raw, caption_embedding_raw, score_sharpness, score_shift_term):
    rows, width = picture_embedding_raw.shape
    n_pool = lax.axis_size("pool")
    result = jax.ShapeDtypeStruct((rows, width), jnp.float32)

    def blocks(count, dtype=jnp.bfloat16):
        return pltpu.VMEM((count * rows, width), dtype)

    vmem = pl.BlockSpec(memory_space=pltpu.VMEM)
    smem = pl.BlockSpec(memory_space=pltpu.SMEM)
    return pl.pallas_call(
        kernel,
        out_shape=(result, result),
        in_specs=[smem, smem, vmem, vmem],
        out_specs=(vmem, vmem),
        scratch_shapes=[
            blocks(n_pool),
            blocks(TEXTS),
            pltpu.VMEM((n_pool * rows, TEXTS * rows), jnp.bfloat16),
            blocks(n_pool, jnp.float32),
            blocks(TEXTS, jnp.float32),
            blocks(n_pool),
            blocks(4),
            blocks(2),
            blocks(5),
            blocks(TEXTS),
            blocks(6),
            pltpu.SemaphoreType.DMA((len(COPIES),)),
            pltpu.SemaphoreType.DMA((len(COPIES),)),
        ],
        compiler_params=pltpu.CompilerParams(
            collective_id=0, has_side_effects=True, vmem_limit_bytes=40 * 2**20
        ),
    )(score_sharpness, score_shift_term, picture_embedding_raw, caption_embedding_raw)

def solution(mesh):
    return jax.shard_map(
        shards,
        mesh=mesh,
        in_specs=(P(("loop", "pool"), None), P(("loop", "pool"), None), P(), P()),
        out_specs=(P(("loop", "pool"), None), P(("loop", "pool"), None)),
        check_vma=False,
    )
```

```python
import jax
import jax.numpy as jnp
from jax import lax
from jax.experimental import pallas as pl
from jax.experimental.pallas import tpu as pltpu
from jax.sharding import PartitionSpec as P

MESH = pl.DeviceIdType.MESH
epsilon_norm = 1e-06

TEXTS = 7
EARLY, FAR = 4, 6

QUARTERS = 4
PARTS = {"A": (0, 2), "B": (2, 2), "A0": (0, 1), "A1": (1, 1), "B0": (2, 1), "B1": (3, 1)}

COPIES = (
    "xA", "xB0", "xB2", "xB3", "xB6", "ownA+", "ownA-", "ownB+", "ownB-", "partA+", "partA-",
    "fwdA+", "fwdA-", "fwdB+", "fwdB-", "pfwdA+", "pfwdA-",
    "tsib", "tfirst", "tsecond", "tfar", "tsib1", "tsib2",
    "xsum7", "xsum4", "xsum5", "xsum1", "xsumA", "phalfA+", "phalfA-", "halfA+", "halfA-", "halfB+", "halfB-",
    "pfullA+0", "pfullA+1", "pfullA-0", "pfullA-1", "fullA+0", "fullA+1", "fullA-0", "fullA-1",
    "fullB+", "fullB-",
    "gsib", "gsib1", "gsib2", "gfirst", "gsecond", "gfar",
)
NUMBER = {name: i for i, name in enumerate(COPIES)}


def inverse_norm(wide):
    return lax.rsqrt(jnp.sum(wide * wide, axis=-1, keepdims=True) + epsilon_norm)


def unit_of(ref):
    wide = ref[...].astype(jnp.float32)
    inverse = inverse_norm(wide)
    return wide * inverse, inverse


def kernel(
    sharp_ref, shift_ref, pic, cap, pic_out, cap_out,
    img, txt, weights, part_sum, tgrad, isend, ixsum, ihalf, ifull, tsend, trecv,
    send_sem, recv_sem,
):
    rows, width = pic.shape
    quarter = rows // QUARTERS
    n_loop = lax.axis_size("loop")
    n_z = n_loop // 4
    group, cls = lax.axis_index("loop"), lax.axis_index("pool")
    sign = 1 - 2 * lax.rem(group, 2)
    z = lax.rem(group // 2, n_z)
    n_y = lax.axis_size("pool") // 2
    x, y = cls // n_y, lax.rem(cls, n_y)
    x_dev = (group, (1 - x) * n_y + y)
    up = (group, x * n_y + lax.rem(y + 1, n_y))
    down = (group, x * n_y + lax.rem(y + n_y - 1, n_y))
    toward = jnp.where(z == n_z - 1, -2, 2)
    first = (lax.rem(group + n_loop + toward, n_loop), cls)
    at_first = jnp.where(z >= n_z - 2, 0, 1)
    across = (z == 0) | (z == n_z - 1)
    at_second = jnp.where(across, 1, 0)
    sibling = (group + sign, cls)
    far_across = jnp.where(sign > 0, z == 0, z == n_z - 1)
    by_first = sign * 2 == toward
    mirror = (1 - x) * n_y + y
    second = (lax.rem(group + n_loop - toward, n_loop), jnp.where(across, mirror, cls))
    far = (lax.rem(group + n_loop - sign, n_loop), jnp.where(far_across, mirror, cls))
    low = z == 0
    beyond = across.astype(jnp.int32) + far_across.astype(jnp.int32)

    barrier = pltpu.get_barrier_semaphore()

    def greet(peer):
        pl.semaphore_signal(barrier, inc=1, device_id=peer, device_id_type=MESH)

    def greet_across():
        @pl.when(across)
        def _():
            greet(second)

        @pl.when(far_across)
        def _():
            greet(far)

    for peer in (x_dev, up, down, first, sibling):
        greet(peer)

    @pl.when(jnp.logical_not(across))
    def _():
        greet(second)

    @pl.when(jnp.logical_not(far_across))
    def _():
        greet(far)

    def block(ref, slot, start=0, size=rows):
        begin = slot * rows + start
        if not isinstance(begin, int):
            begin = pl.multiple_of(begin, rows)
        return ref.at[pl.ds(begin, size)]

    copies = {}

    def make(name, src, dst, device, lands=0):
        n = NUMBER[name]
        copies[name] = pltpu.make_async_remote_copy(
            src_ref=src, dst_ref=dst, send_sem=send_sem.at[n], recv_sem=recv_sem.at[n + lands],
            device_id=device, device_id_type=MESH,
        )
        return copies[name]

    def send(name, src, dst, device, lands=0):
        make(name, src, dst, device, lands).start()

    def arrived(*names):
        for name in names:
            copies[name].wait_recv()

    def came(name, dst):
        n = NUMBER[name]
        pltpu.make_async_remote_copy(
            src_ref=dst, dst_ref=dst, send_sem=send_sem.at[n], recv_sem=recv_sem.at[n],
            device_id=first, device_id_type=MESH,
        ).wait_recv()

    img[0:rows] = unit_of(pic)[0].astype(jnp.bfloat16)
    txt[0:rows] = unit_of(cap)[0].astype(jnp.bfloat16)
    sharp, shift = sharp_ref[0], shift_ref[0]

    pl.semaphore_wait(barrier, jnp.where(low, 7 - beyond, 7))
    greet_across()

    def place(part):
        first_quarter, count = PARTS[part]
        return first_quarter * quarter, count * quarter

    def piece(ref, slot, part):
        return block(ref, slot, *place(part))

    def move(name, part, ref, slot, dst, dst_slot, device):
        send(name, piece(ref, slot, part), piece(dst, dst_slot, part), device)

    move("xA", "A", img, 0, img, 1, x_dev)
    move("ownB+", "B", img, 0, img, 3, up)
    move("ownB-", "B", img, 0, img, 2, down)
    send("tsib", block(txt, 0), block(txt, 1), sibling)
    make("tsecond", block(txt, 0), block(txt, 2 + 2 * at_second), second, at_second - 1)
    make("tfar", block(txt, jnp.where(by_first, 2, 4)), block(txt, 6), far)

    @pl.when(jnp.logical_not(low & across))
    def _():
        copies["tsecond"].start()

    send("tfirst", block(txt, 0), block(txt, 2 + 2 * at_first), first, at_first)
    move("ownA+", "A", img, 0, img, 3, up)
    move("ownA-", "A", img, 0, img, 2, down)
    move("xB0", "B", img, 0, img, 1, x_dev)

    arrived("ownB+", "ownB-")
    move("fwdB+", "B0", img, 3, img, 6, up)
    move("fwdB-", "B1", img, 2, img, 6, down)
    move("xB2", "B", img, 2, img, 4, x_dev)
    move("xB3", "B", img, 3, img, 5, x_dev)
    arrived("xA")
    move("partA+", "A", img, 1, img, 5, up)
    move("partA-", "A", img, 1, img, 4, down)
    arrived("ownA+", "ownA-")
    move("fwdA+", "A0", img, 3, img, 6, up)
    move("fwdA-", "A1", img, 2, img, 6, down)
    came("tfirst", block(txt, 2))
    send("tsib1", block(txt, 2), block(txt, 3), sibling)

    @pl.when(by_first & jnp.logical_not(low & far_across))
    def _():
        copies["tfar"].start()

    arrived("fwdB+", "fwdB-")
    move("xB6", "B", img, 6, img, 7, x_dev)
    make("tsib2", block(txt, 4), block(txt, 5), sibling)

    def second_text():
        came("tsecond", block(txt, 4))
        copies["tsib2"].start()

        @pl.when(jnp.logical_not(by_first))
        def _():
            copies["tfar"].start()

    @pl.when(jnp.logical_not(across))
    def _():
        second_text()

    arrived("xB0", "tsib", "tsib1")

    def score(slot, count, begin, end):
        here = pl.ds(slot * rows, count * rows)
        dots = lax.dot_general(
            img[here], txt[begin * rows : end * rows], (((1,), (1,)), ((), ())),
            preferred_element_type=jnp.float32,
        )
        chance = 1.0 / (1.0 + jnp.exp(-(sharp * dots + shift)))
        if slot == 0 and begin == 0:
            i = lax.broadcasted_iota(jnp.int32, chance.shape, 0)
            j = lax.broadcasted_iota(jnp.int32, chance.shape, 1)
            chance = chance - ((i == j) & (i < rows)).astype(jnp.float32)
        weights[here, begin * rows : end * rows] = (sharp * chance).astype(jnp.bfloat16)

    def image_grad(slot, count):
        here = pl.ds(slot * rows, count * rows)
        part_sum[here] = jnp.dot(weights[here], txt[...], preferred_element_type=jnp.float32)

    def text_grad(begin, end):
        tgrad[begin * rows : end * rows] = lax.dot_general(
            weights[:, begin * rows : end * rows], img[...], (((0,), (0,)), ((), ())),
            preferred_element_type=jnp.float32,
        )

    def take(slot, part):
        start, size = place(part)
        return part_rows(part_sum, slot, start, size)

    def part_rows(ref, slot, start, size):
        return ref[slot * rows + start : slot * rows + start + size]

    def put(slot, part, *extra):
        start, size = place(part)
        value = take(slot, part)
        for ref, ref_slot in extra:
            value = value + part_rows(ref, ref_slot, start, size).astype(jnp.float32)
        isend[slot * rows + start : slot * rows + start + size] = value.astype(jnp.bfloat16)

    score(0, 4, 0, EARLY)

    @pl.when(low & (beyond > 0))
    def _():
        pl.semaphore_wait(barrier, beyond)

        @pl.when(across)
        def _():
            copies["tsecond"].start()

        @pl.when(far_across)
        def _():
            copies["tfar"].start()

    arrived("partA+", "partA-")
    move("pfwdA+", "A0", img, 5, img, 7, up)
    move("pfwdA-", "A1", img, 4, img, 7, down)

    arrived("xB2", "xB3")
    score(4, 2, 0, EARLY)

    @pl.when(across)
    def _():
        second_text()

    arrived("tsib2")
    score(0, 4, EARLY, FAR)
    score(4, 2, EARLY, FAR)
    arrived("fwdA+", "fwdA-", "pfwdA+", "pfwdA-", "xB6")
    score(6, 2, 0, FAR)
    arrived("tfar")
    score(6, 2, FAR, TEXTS)
    image_grad(6, 2)
    put(7, "B")
    move("xsum7", "B", isend, 7, ixsum, 3, x_dev)
    put(7, "A")
    move("phalfA+", "A0", isend, 7, ihalf, 0, up)
    move("phalfA-", "A1", isend, 7, ihalf, 0, down)
    put(6, "A")
    move("halfA+", "A0", isend, 6, ihalf, 1, up)
    move("halfA-", "A1", isend, 6, ihalf, 1, down)

    def grad_rows(slot):
        return tgrad[slot * rows : (slot + 1) * rows]

    def put_text(n, value):
        tsend[n * rows : (n + 1) * rows] = value.astype(jnp.bfloat16)

    def got_text(n):
        return trecv[n * rows : (n + 1) * rows].astype(jnp.float32)

    score(0, 6, FAR, TEXTS)
    text_grad(FAR, TEXTS)
    put_text(6, grad_rows(6))
    send("gfar", block(tsend, 6), block(trecv, 5), far)
    text_grad(EARLY, FAR)
    put_text(5, grad_rows(5))
    send("gsib2", block(tsend, 5), block(trecv, 2), sibling)

    image_grad(4, 2)
    put(4, "B")
    move("xsum4", "B", isend, 4, ixsum, 1, x_dev)
    put(5, "B")
    move("xsum5", "B", isend, 5, ixsum, 2, x_dev)
    put(4, "A1")
    move("pfullA+1", "A1", isend, 4, ifull, 0, up)
    put(5, "A0")
    move("pfullA-0", "A0", isend, 5, ifull, 1, down)

    arrived("phalfA+", "phalfA-")
    put(4, "A0", (ihalf, 0))
    move("pfullA+0", "A0", isend, 4, ifull, 0, up)
    put(5, "A1", (ihalf, 0))
    move("pfullA-1", "A1", isend, 5, ifull, 1, down)

    image_grad(0, 4)
    put(1, "B")
    move("xsum1", "B", isend, 1, ixsum, 0, x_dev)
    put(2, "A1")
    move("fullA+1", "A1", isend, 2, ifull, 2, up)
    put(3, "A0")
    move("fullA-0", "A0", isend, 3, ifull, 3, down)
    arrived("halfA+", "halfA-")
    put(2, "A0", (ihalf, 1))
    move("fullA+0", "A0", isend, 2, ifull, 2, up)
    put(3, "A1", (ihalf, 1))
    move("fullA-1", "A1", isend, 3, ifull, 3, down)

    arrived("xsum7")
    put(6, "B", (ixsum, 3))
    move("halfB+", "B0", isend, 6, ihalf, 1, up)
    move("halfB-", "B1", isend, 6, ihalf, 1, down)

    def pass_back(name, slot, other, more):
        @pl.when(more)
        def _():
            arrived("gfar")
            put_text(slot, grad_rows(slot) + got_text(other) + got_text(5))

        @pl.when(jnp.logical_not(more))
        def _():
            put_text(slot, grad_rows(slot) + got_text(other))

        copies[name].start()

    make("gfirst", block(tsend, 2), block(trecv, 3 + at_first), first, at_first)
    make("gsecond", block(tsend, 4), block(trecv, 3 + at_second), second, at_second - 1)

    arrived("gsib2")
    pass_back("gsecond", 4, 2, jnp.logical_not(by_first))

    text_grad(0, EARLY)
    put_text(3, grad_rows(3))
    send("gsib1", block(tsend, 3), block(trecv, 1), sibling)
    put_text(1, grad_rows(1))
    send("gsib", block(tsend, 1), block(trecv, 0), sibling)

    arrived("pfullA+0", "pfullA+1", "pfullA-0", "pfullA-1")
    put(1, "A", (ifull, 0), (ifull, 1))
    move("xsumA", "A", isend, 1, ifull, 4, x_dev)

    arrived("gsib1")

    def pass_first():
        pass_back("gfirst", 2, 1, by_first)

    @pl.when(jnp.logical_not(low & far_across))
    def _():
        pass_first()

    arrived("xsum4", "xsum5", "halfB+", "halfB-")
    put(2, "B0", (ixsum, 1), (ihalf, 1))
    put(2, "B1", (ixsum, 1))
    move("fullB+", "B", isend, 2, ifull, 2, up)
    put(3, "B0", (ixsum, 2))
    put(3, "B1", (ixsum, 2), (ihalf, 1))
    move("fullB-", "B", isend, 3, ifull, 3, down)

    @pl.when(low & far_across)
    def _():
        pass_first()

    def got_full(n):
        return ifull[n * rows : (n + 1) * rows].astype(jnp.float32)

    arrived("gsib")
    came("gfirst", block(trecv, 3))
    came("gsecond", block(trecv, 4))
    def back(ref, grad):
        unit, inverse = unit_of(ref)
        return inverse * (grad - unit * jnp.sum(unit * grad, axis=-1, keepdims=True))

    cap_hat_grad = grad_rows(0) + got_text(0) + got_text(3) + got_text(4)
    cap_out[...] = back(cap, cap_hat_grad)

    arrived("fullA+0", "fullA+1", "fullA-0", "fullA-1", "xsumA", "xsum1", "fullB+", "fullB-")
    size = place("A")[1]
    crossed = (got_full(4)[:size], ixsum[size : 2 * size].astype(jnp.float32))
    pic_hat_grad = part_sum[0:rows] + got_full(2) + got_full(3) + jnp.concatenate(crossed, axis=0)
    pic_out[...] = back(pic, pic_hat_grad)

    for name in COPIES:
        copies[name].wait_send()


def shards(picture_embedding_raw, caption_embedding_raw, score_sharpness, score_shift_term):
    rows, width = picture_embedding_raw.shape
    n_pool = lax.axis_size("pool")
    result = jax.ShapeDtypeStruct((rows, width), jnp.float32)

    def blocks(count, dtype=jnp.bfloat16):
        return pltpu.VMEM((count * rows, width), dtype)

    vmem = pl.BlockSpec(memory_space=pltpu.VMEM)
    smem = pl.BlockSpec(memory_space=pltpu.SMEM)
    return pl.pallas_call(
        kernel,
        out_shape=(result, result),
        in_specs=[smem, smem, vmem, vmem],
        out_specs=(vmem, vmem),
        scratch_shapes=[
            blocks(n_pool),
            blocks(TEXTS),
            pltpu.VMEM((n_pool * rows, TEXTS * rows), jnp.bfloat16),
            blocks(n_pool, jnp.float32),
            blocks(TEXTS, jnp.float32),
            blocks(n_pool),
            blocks(4),
            blocks(2),
            blocks(5),
            blocks(TEXTS),
            blocks(6),
            pltpu.SemaphoreType.DMA((len(COPIES),)),
            pltpu.SemaphoreType.DMA((len(COPIES),)),
        ],
        compiler_params=pltpu.CompilerParams(
            collective_id=0, has_side_effects=True, vmem_limit_bytes=40 * 2**20
        ),
    )(score_sharpness, score_shift_term, picture_embedding_raw, caption_embedding_raw)

def solution(mesh):
    return jax.shard_map(
        shards,
        mesh=mesh,
        in_specs=(P(("loop", "pool"), None), P(("loop", "pool"), None), P(), P()),
        out_specs=(P(("loop", "pool"), None), P(("loop", "pool"), None)),
        check_vma=False,
    )
```

```python
import jax
import jax.numpy as jnp
from jax import lax
from jax.experimental import pallas as pl
from jax.experimental.pallas import tpu as pltpu
from jax.sharding import PartitionSpec as P

MESH = pl.DeviceIdType.MESH
epsilon_norm = 1e-06

TEXTS = 7
EARLY, FAR = 4, 6

QUARTERS = 4
PARTS = {"A": (0, 2), "B": (2, 2), "A0": (0, 1), "A1": (1, 1), "B0": (2, 1), "B1": (3, 1)}

COPIES = (
    "xA", "xB0", "xB2", "xB3", "xB6", "ownA+", "ownA-", "ownB+", "ownB-", "partA+", "partA-",
    "fwdA+", "fwdA-", "fwdB+", "fwdB-", "pfwdA+", "pfwdA-",
    "tsib", "tfirst", "tsecond", "tfar", "tsib1", "tsib2",
    "xsum7", "xsum4", "xsum5", "xsum1", "xsumA", "phalfA+", "phalfA-", "halfA+", "halfA-", "halfB+", "halfB-",
    "pfullA+0", "pfullA+1", "pfullA-0", "pfullA-1", "fullA+0", "fullA+1", "fullA-0", "fullA-1",
    "fullB+", "fullB-",
    "gsib", "gsib1", "gsib2", "gfirst", "gsecond", "gfar",
)
NUMBER = {name: i for i, name in enumerate(COPIES)}


def inverse_norm(wide):
    return lax.rsqrt(jnp.sum(wide * wide, axis=-1, keepdims=True) + epsilon_norm)


def unit_of(ref):
    wide = ref[...].astype(jnp.float32)
    inverse = inverse_norm(wide)
    return wide * inverse, inverse


def kernel(
    sharp_ref, shift_ref, pic, cap, pic_out, cap_out,
    img, txt, weights, part_sum, tgrad, isend, ixsum, ihalf, ifull, tsend, trecv,
    send_sem, recv_sem,
):
    rows, width = pic.shape
    quarter = rows // QUARTERS
    n_loop = lax.axis_size("loop")
    n_z = n_loop // 4
    group, cls = lax.axis_index("loop"), lax.axis_index("pool")
    sign = 1 - 2 * lax.rem(group, 2)
    z = lax.rem(group // 2, n_z)
    n_y = lax.axis_size("pool") // 2
    x, y = cls // n_y, lax.rem(cls, n_y)
    x_dev = (group, (1 - x) * n_y + y)
    up = (group, x * n_y + lax.rem(y + 1, n_y))
    down = (group, x * n_y + lax.rem(y + n_y - 1, n_y))
    toward = jnp.where(z == n_z - 1, -2, 2)
    first = (lax.rem(group + n_loop + toward, n_loop), cls)
    at_first = jnp.where(z >= n_z - 2, 0, 1)
    across = (z == 0) | (z == n_z - 1)
    at_second = jnp.where(across, 1, 0)
    sibling = (group + sign, cls)
    far_across = jnp.where(sign > 0, z == 0, z == n_z - 1)
    by_first = sign * 2 == toward
    mirror = (1 - x) * n_y + y
    second = (lax.rem(group + n_loop - toward, n_loop), jnp.where(across, mirror, cls))
    far = (lax.rem(group + n_loop - sign, n_loop), jnp.where(far_across, mirror, cls))
    low = z == 0
    beyond = across.astype(jnp.int32) + far_across.astype(jnp.int32)

    barrier = pltpu.get_barrier_semaphore()

    def greet(peer):
        pl.semaphore_signal(barrier, inc=1, device_id=peer, device_id_type=MESH)

    def greet_across():
        @pl.when(across)
        def _():
            greet(second)

        @pl.when(far_across)
        def _():
            greet(far)

    for peer in (x_dev, up, down, first, sibling):
        greet(peer)

    @pl.when(jnp.logical_not(across))
    def _():
        greet(second)

    @pl.when(jnp.logical_not(far_across))
    def _():
        greet(far)

    def block(ref, slot, start=0, size=rows):
        begin = slot * rows + start
        if not isinstance(begin, int):
            begin = pl.multiple_of(begin, rows)
        return ref.at[pl.ds(begin, size)]

    copies = {}

    def make(name, src, dst, device, lands=0):
        n = NUMBER[name]
        copies[name] = pltpu.make_async_remote_copy(
            src_ref=src, dst_ref=dst, send_sem=send_sem.at[n], recv_sem=recv_sem.at[n + lands],
            device_id=device, device_id_type=MESH,
        )
        return copies[name]

    def send(name, src, dst, device, lands=0):
        make(name, src, dst, device, lands).start()

    def arrived(*names):
        for name in names:
            copies[name].wait_recv()

    def came(name, dst):
        n = NUMBER[name]
        pltpu.make_async_remote_copy(
            src_ref=dst, dst_ref=dst, send_sem=send_sem.at[n], recv_sem=recv_sem.at[n],
            device_id=first, device_id_type=MESH,
        ).wait_recv()

    img[0:rows] = unit_of(pic)[0].astype(jnp.bfloat16)
    txt[0:rows] = unit_of(cap)[0].astype(jnp.bfloat16)
    sharp, shift = sharp_ref[0], shift_ref[0]

    pl.semaphore_wait(barrier, jnp.where(low, 7 - beyond, 7))
    greet_across()

    def place(part):
        first_quarter, count = PARTS[part]
        return first_quarter * quarter, count * quarter

    def piece(ref, slot, part):
        return block(ref, slot, *place(part))

    def move(name, part, ref, slot, dst, dst_slot, device):
        send(name, piece(ref, slot, part), piece(dst, dst_slot, part), device)

    move("xA", "A", img, 0, img, 1, x_dev)
    move("ownB+", "B", img, 0, img, 3, up)
    move("ownB-", "B", img, 0, img, 2, down)
    send("tsib", block(txt, 0), block(txt, 1), sibling)
    make("tsecond", block(txt, 0), block(txt, 2 + 2 * at_second), second, at_second - 1)
    make("tfar", block(txt, jnp.where(by_first, 2, 4)), block(txt, 6), far)

    @pl.when(jnp.logical_not(low & across))
    def _():
        copies["tsecond"].start()

    send("tfirst", block(txt, 0), block(txt, 2 + 2 * at_first), first, at_first)
    move("ownA+", "A", img, 0, img, 3, up)
    move("ownA-", "A", img, 0, img, 2, down)
    move("xB0", "B", img, 0, img, 1, x_dev)

    arrived("ownB+", "ownB-")
    move("fwdB+", "B0", img, 3, img, 6, up)
    move("fwdB-", "B1", img, 2, img, 6, down)
    move("xB2", "B", img, 2, img, 4, x_dev)
    move("xB3", "B", img, 3, img, 5, x_dev)
    arrived("xA")
    move("partA+", "A", img, 1, img, 5, up)
    move("partA-", "A", img, 1, img, 4, down)
    arrived("ownA+", "ownA-")
    move("fwdA+", "A0", img, 3, img, 6, up)
    move("fwdA-", "A1", img, 2, img, 6, down)
    came("tfirst", block(txt, 2))
    send("tsib1", block(txt, 2), block(txt, 3), sibling)

    @pl.when(by_first & jnp.logical_not(low & far_across))
    def _():
        copies["tfar"].start()

    arrived("fwdB+", "fwdB-")
    move("xB6", "B", img, 6, img, 7, x_dev)
    make("tsib2", block(txt, 4), block(txt, 5), sibling)

    def second_text():
        came("tsecond", block(txt, 4))
        copies["tsib2"].start()

        @pl.when(jnp.logical_not(by_first))
        def _():
            copies["tfar"].start()

    @pl.when(jnp.logical_not(across))
    def _():
        second_text()

    arrived("xB0", "tsib", "tsib1")

    def score(slot, count, begin, end):
        here = pl.ds(slot * rows, count * rows)
        dots = lax.dot_general(
            img[here], txt[begin * rows : end * rows], (((1,), (1,)), ((), ())),
            preferred_element_type=jnp.float32,
        )
        chance = 1.0 / (1.0 + jnp.exp(-(sharp * dots + shift)))
        if slot == 0 and begin == 0:
            i = lax.broadcasted_iota(jnp.int32, chance.shape, 0)
            j = lax.broadcasted_iota(jnp.int32, chance.shape, 1)
            chance = chance - ((i == j) & (i < rows)).astype(jnp.float32)
        weights[here, begin * rows : end * rows] = (sharp * chance).astype(jnp.bfloat16)

    def image_grad(slot, count):
        here = pl.ds(slot * rows, count * rows)
        part_sum[here] = jnp.dot(weights[here], txt[...], preferred_element_type=jnp.float32)

    def text_grad(begin, end):
        tgrad[begin * rows : end * rows] = lax.dot_general(
            weights[:, begin * rows : end * rows], img[...], (((0,), (0,)), ((), ())),
            preferred_element_type=jnp.float32,
        )

    def take(slot, part):
        start, size = place(part)
        return part_rows(part_sum, slot, start, size)

    def part_rows(ref, slot, start, size):
        return ref[slot * rows + start : slot * rows + start + size]

    def put(slot, part, *extra):
        start, size = place(part)
        value = take(slot, part)
        for ref, ref_slot in extra:
            value = value + part_rows(ref, ref_slot, start, size).astype(jnp.float32)
        isend[slot * rows + start : slot * rows + start + size] = value.astype(jnp.bfloat16)

    @pl.when(low & (beyond > 0))
    def _():
        pl.semaphore_wait(barrier, beyond)

        @pl.when(across)
        def _():
            copies["tsecond"].start()

        @pl.when(far_across)
        def _():
            copies["tfar"].start()

    score(0, 4, 0, EARLY)

    arrived("partA+", "partA-")
    move("pfwdA+", "A0", img, 5, img, 7, up)
    move("pfwdA-", "A1", img, 4, img, 7, down)

    @pl.when(across & jnp.logical_not(low))
    def _():
        second_text()

    arrived("xB2", "xB3")
    score(4, 2, 0, EARLY)

    @pl.when(low & across)
    def _():
        second_text()

    arrived("tsib2")
    score(0, 4, EARLY, FAR)
    score(4, 2, EARLY, FAR)
    arrived("fwdA+", "fwdA-", "pfwdA+", "pfwdA-", "xB6")
    score(6, 2, 0, FAR)
    arrived("tfar")
    score(6, 2, FAR, TEXTS)
    image_grad(6, 2)
    put(7, "B")
    move("xsum7", "B", isend, 7, ixsum, 3, x_dev)
    put(7, "A")
    move("phalfA+", "A0", isend, 7, ihalf, 0, up)
    move("phalfA-", "A1", isend, 7, ihalf, 0, down)
    put(6, "A")
    move("halfA+", "A0", isend, 6, ihalf, 1, up)
    move("halfA-", "A1", isend, 6, ihalf, 1, down)

    def grad_rows(slot):
        return tgrad[slot * rows : (slot + 1) * rows]

    def put_text(n, value):
        tsend[n * rows : (n + 1) * rows] = value.astype(jnp.bfloat16)

    def got_text(n):
        return trecv[n * rows : (n + 1) * rows].astype(jnp.float32)

    score(0, 6, FAR, TEXTS)
    text_grad(FAR, TEXTS)
    put_text(6, grad_rows(6))
    send("gfar", block(tsend, 6), block(trecv, 5), far)
    text_grad(EARLY, FAR)
    put_text(5, grad_rows(5))
    send("gsib2", block(tsend, 5), block(trecv, 2), sibling)

    image_grad(4, 2)
    put(4, "B")
    move("xsum4", "B", isend, 4, ixsum, 1, x_dev)
    put(5, "B")
    move("xsum5", "B", isend, 5, ixsum, 2, x_dev)
    put(4, "A1")
    move("pfullA+1", "A1", isend, 4, ifull, 0, up)
    put(5, "A0")
    move("pfullA-0", "A0", isend, 5, ifull, 1, down)

    arrived("phalfA+", "phalfA-")
    put(4, "A0", (ihalf, 0))
    move("pfullA+0", "A0", isend, 4, ifull, 0, up)
    put(5, "A1", (ihalf, 0))
    move("pfullA-1", "A1", isend, 5, ifull, 1, down)

    image_grad(0, 4)
    put(1, "B")
    move("xsum1", "B", isend, 1, ixsum, 0, x_dev)
    put(2, "A1")
    move("fullA+1", "A1", isend, 2, ifull, 2, up)
    put(3, "A0")
    move("fullA-0", "A0", isend, 3, ifull, 3, down)
    arrived("halfA+", "halfA-")
    put(2, "A0", (ihalf, 1))
    move("fullA+0", "A0", isend, 2, ifull, 2, up)
    put(3, "A1", (ihalf, 1))
    move("fullA-1", "A1", isend, 3, ifull, 3, down)

    arrived("xsum7")
    put(6, "B", (ixsum, 3))
    move("halfB+", "B0", isend, 6, ihalf, 1, up)
    move("halfB-", "B1", isend, 6, ihalf, 1, down)

    def pass_back(name, slot, other, more):
        @pl.when(more)
        def _():
            arrived("gfar")
            put_text(slot, grad_rows(slot) + got_text(other) + got_text(5))

        @pl.when(jnp.logical_not(more))
        def _():
            put_text(slot, grad_rows(slot) + got_text(other))

        copies[name].start()

    make("gfirst", block(tsend, 2), block(trecv, 3 + at_first), first, at_first)
    make("gsecond", block(tsend, 4), block(trecv, 3 + at_second), second, at_second - 1)

    arrived("gsib2")
    pass_back("gsecond", 4, 2, jnp.logical_not(by_first))

    text_grad(0, EARLY)
    put_text(3, grad_rows(3))
    send("gsib1", block(tsend, 3), block(trecv, 1), sibling)
    put_text(1, grad_rows(1))
    send("gsib", block(tsend, 1), block(trecv, 0), sibling)

    arrived("pfullA+0", "pfullA+1", "pfullA-0", "pfullA-1")
    put(1, "A", (ifull, 0), (ifull, 1))
    move("xsumA", "A", isend, 1, ifull, 4, x_dev)

    arrived("gsib1")

    def pass_first():
        pass_back("gfirst", 2, 1, by_first)

    @pl.when(jnp.logical_not(low & far_across))
    def _():
        pass_first()

    arrived("xsum4", "xsum5", "halfB+", "halfB-")
    put(2, "B0", (ixsum, 1), (ihalf, 1))
    put(2, "B1", (ixsum, 1))
    move("fullB+", "B", isend, 2, ifull, 2, up)
    put(3, "B0", (ixsum, 2))
    put(3, "B1", (ixsum, 2), (ihalf, 1))
    move("fullB-", "B", isend, 3, ifull, 3, down)

    @pl.when(low & far_across)
    def _():
        pass_first()

    def got_full(n):
        return ifull[n * rows : (n + 1) * rows].astype(jnp.float32)

    arrived("gsib")
    came("gfirst", block(trecv, 3))
    came("gsecond", block(trecv, 4))
    def back(ref, grad):
        unit, inverse = unit_of(ref)
        return inverse * (grad - unit * jnp.sum(unit * grad, axis=-1, keepdims=True))

    cap_hat_grad = grad_rows(0) + got_text(0) + got_text(3) + got_text(4)
    cap_out[...] = back(cap, cap_hat_grad)

    arrived("fullA+0", "fullA+1", "fullA-0", "fullA-1", "xsumA", "xsum1", "fullB+", "fullB-")
    size = place("A")[1]
    crossed = (got_full(4)[:size], ixsum[size : 2 * size].astype(jnp.float32))
    pic_hat_grad = part_sum[0:rows] + got_full(2) + got_full(3) + jnp.concatenate(crossed, axis=0)
    pic_out[...] = back(pic, pic_hat_grad)

    for name in COPIES:
        copies[name].wait_send()


def shards(picture_embedding_raw, caption_embedding_raw, score_sharpness, score_shift_term):
    rows, width = picture_embedding_raw.shape
    n_pool = lax.axis_size("pool")
    result = jax.ShapeDtypeStruct((rows, width), jnp.float32)

    def blocks(count, dtype=jnp.bfloat16):
        return pltpu.VMEM((count * rows, width), dtype)

    vmem = pl.BlockSpec(memory_space=pltpu.VMEM)
    smem = pl.BlockSpec(memory_space=pltpu.SMEM)
    return pl.pallas_call(
        kernel,
        out_shape=(result, result),
        in_specs=[smem, smem, vmem, vmem],
        out_specs=(vmem, vmem),
        scratch_shapes=[
            blocks(n_pool),
            blocks(TEXTS),
            pltpu.VMEM((n_pool * rows, TEXTS * rows), jnp.bfloat16),
            blocks(n_pool, jnp.float32),
            blocks(TEXTS, jnp.float32),
            blocks(n_pool),
            blocks(4),
            blocks(2),
            blocks(5),
            blocks(TEXTS),
            blocks(6),
            pltpu.SemaphoreType.DMA((len(COPIES),)),
            pltpu.SemaphoreType.DMA((len(COPIES),)),
        ],
        compiler_params=pltpu.CompilerParams(
            collective_id=0, has_side_effects=True, vmem_limit_bytes=40 * 2**20
        ),
    )(score_sharpness, score_shift_term, picture_embedding_raw, caption_embedding_raw)

def solution(mesh):
    return jax.shard_map(
        shards,
        mesh=mesh,
        in_specs=(P(("loop", "pool"), None), P(("loop", "pool"), None), P(), P()),
        out_specs=(P(("loop", "pool"), None), P(("loop", "pool"), None)),
        check_vma=False,
    )
```

```python
import jax
import jax.numpy as jnp
from jax import lax
from jax.experimental import pallas as pl
from jax.experimental.pallas import tpu as pltpu
from jax.sharding import PartitionSpec as P

MESH = pl.DeviceIdType.MESH
epsilon_norm = 1e-06

TEXTS = 7
EARLY, FAR = 4, 6

QUARTERS = 4
PARTS = {"A": (0, 2), "B": (2, 2), "A0": (0, 1), "A1": (1, 1), "B0": (2, 1), "B1": (3, 1)}

COPIES = (
    "xA", "xB0", "xB2", "xB3", "xB6", "ownA+", "ownA-", "ownB+", "ownB-", "partA+", "partA-",
    "fwdA+", "fwdA-", "fwdB+", "fwdB-", "pfwdA+", "pfwdA-",
    "tsib", "tfirst", "tsecond", "tfar", "tsib1", "tsib2",
    "xsum7", "xsum4", "xsum5", "xsum1", "xsumA", "phalfA+", "phalfA-", "halfA+", "halfA-", "halfB+", "halfB-",
    "pfullA+0", "pfullA+1", "pfullA-0", "pfullA-1", "fullA+0", "fullA+1", "fullA-0", "fullA-1",
    "fullB+", "fullB-",
    "gsib", "gsib1", "gsib2", "gfirst", "gsecond", "gfar",
)
NUMBER = {name: i for i, name in enumerate(COPIES)}


def inverse_norm(wide):
    return lax.rsqrt(jnp.sum(wide * wide, axis=-1, keepdims=True) + epsilon_norm)


def unit_of(ref):
    wide = ref[...].astype(jnp.float32)
    inverse = inverse_norm(wide)
    return wide * inverse, inverse


def kernel(
    sharp_ref, shift_ref, pic, cap, pic_out, cap_out,
    img, txt, weights, part_sum, tgrad, isend, ixsum, ihalf, ifull, tsend, trecv,
    send_sem, recv_sem,
):
    rows, width = pic.shape
    quarter = rows // QUARTERS
    n_loop = lax.axis_size("loop")
    n_z = n_loop // 4
    group, cls = lax.axis_index("loop"), lax.axis_index("pool")
    sign = 1 - 2 * lax.rem(group, 2)
    z = lax.rem(group // 2, n_z)
    n_y = lax.axis_size("pool") // 2
    x, y = cls // n_y, lax.rem(cls, n_y)
    x_dev = (group, (1 - x) * n_y + y)
    up = (group, x * n_y + lax.rem(y + 1, n_y))
    down = (group, x * n_y + lax.rem(y + n_y - 1, n_y))
    toward = jnp.where(z == n_z - 1, -2, 2)
    first = (lax.rem(group + n_loop + toward, n_loop), cls)
    at_first = jnp.where(z >= n_z - 2, 0, 1)
    across = (z == 0) | (z == n_z - 1)
    at_second = jnp.where(across, 1, 0)
    sibling = (group + sign, cls)
    far_across = jnp.where(sign > 0, z == 0, z == n_z - 1)
    by_first = sign * 2 == toward
    mirror = (1 - x) * n_y + y
    second = (lax.rem(group + n_loop - toward, n_loop), jnp.where(across, mirror, cls))
    far = (lax.rem(group + n_loop - sign, n_loop), jnp.where(far_across, mirror, cls))
    low = z == 0
    beyond = across.astype(jnp.int32) + far_across.astype(jnp.int32)

    barrier = pltpu.get_barrier_semaphore()

    def greet(peer):
        pl.semaphore_signal(barrier, inc=1, device_id=peer, device_id_type=MESH)

    def greet_across():
        @pl.when(across)
        def _():
            greet(second)

        @pl.when(far_across)
        def _():
            greet(far)

    for peer in (x_dev, up, down, first, sibling):
        greet(peer)

    @pl.when(jnp.logical_not(across))
    def _():
        greet(second)

    @pl.when(jnp.logical_not(far_across))
    def _():
        greet(far)

    def block(ref, slot, start=0, size=rows):
        begin = slot * rows + start
        if not isinstance(begin, int):
            begin = pl.multiple_of(begin, rows)
        return ref.at[pl.ds(begin, size)]

    copies = {}

    def make(name, src, dst, device, lands=0):
        n = NUMBER[name]
        copies[name] = pltpu.make_async_remote_copy(
            src_ref=src, dst_ref=dst, send_sem=send_sem.at[n], recv_sem=recv_sem.at[n + lands],
            device_id=device, device_id_type=MESH,
        )
        return copies[name]

    def send(name, src, dst, device, lands=0):
        make(name, src, dst, device, lands).start()

    def arrived(*names):
        for name in names:
            copies[name].wait_recv()

    def came(name, dst):
        n = NUMBER[name]
        pltpu.make_async_remote_copy(
            src_ref=dst, dst_ref=dst, send_sem=send_sem.at[n], recv_sem=recv_sem.at[n],
            device_id=first, device_id_type=MESH,
        ).wait_recv()

    img[0:rows] = unit_of(pic)[0].astype(jnp.bfloat16)
    txt[0:rows] = unit_of(cap)[0].astype(jnp.bfloat16)
    sharp, shift = sharp_ref[0], shift_ref[0]

    pl.semaphore_wait(barrier, jnp.where(low, 7 - beyond, 7))
    greet_across()

    def place(part):
        first_quarter, count = PARTS[part]
        return first_quarter * quarter, count * quarter

    def piece(ref, slot, part):
        return block(ref, slot, *place(part))

    def move(name, part, ref, slot, dst, dst_slot, device):
        send(name, piece(ref, slot, part), piece(dst, dst_slot, part), device)

    move("xA", "A", img, 0, img, 1, x_dev)
    move("ownB+", "B", img, 0, img, 3, up)
    move("ownB-", "B", img, 0, img, 2, down)
    send("tsib", block(txt, 0), block(txt, 1), sibling)
    make("tsecond", block(txt, 0), block(txt, 2 + 2 * at_second), second, at_second - 1)
    make("tfar", block(txt, jnp.where(by_first, 2, 4)), block(txt, 6), far)

    @pl.when(jnp.logical_not(low & across))
    def _():
        copies["tsecond"].start()

    send("tfirst", block(txt, 0), block(txt, 2 + 2 * at_first), first, at_first)
    move("ownA+", "A", img, 0, img, 3, up)
    move("ownA-", "A", img, 0, img, 2, down)
    move("xB0", "B", img, 0, img, 1, x_dev)

    arrived("ownB+", "ownB-")
    move("fwdB+", "B0", img, 3, img, 6, up)
    move("fwdB-", "B1", img, 2, img, 6, down)
    move("xB2", "B", img, 2, img, 4, x_dev)
    move("xB3", "B", img, 3, img, 5, x_dev)
    arrived("xA")
    move("partA+", "A", img, 1, img, 5, up)
    move("partA-", "A", img, 1, img, 4, down)
    arrived("ownA+", "ownA-")
    move("fwdA+", "A0", img, 3, img, 6, up)
    move("fwdA-", "A1", img, 2, img, 6, down)
    came("tfirst", block(txt, 2))
    send("tsib1", block(txt, 2), block(txt, 3), sibling)

    @pl.when(by_first & jnp.logical_not(low & far_across))
    def _():
        copies["tfar"].start()

    arrived("fwdB+", "fwdB-")
    move("xB6", "B", img, 6, img, 7, x_dev)
    make("tsib2", block(txt, 4), block(txt, 5), sibling)

    def second_text():
        came("tsecond", block(txt, 4))
        copies["tsib2"].start()

        @pl.when(jnp.logical_not(by_first))
        def _():
            copies["tfar"].start()

    @pl.when(jnp.logical_not(across))
    def _():
        second_text()

    arrived("xB0", "tsib", "tsib1")

    def score(slot, count, begin, end):
        here = pl.ds(slot * rows, count * rows)
        dots = lax.dot_general(
            img[here], txt[begin * rows : end * rows], (((1,), (1,)), ((), ())),
            preferred_element_type=jnp.float32,
        )
        chance = 1.0 / (1.0 + jnp.exp(-(sharp * dots + shift)))
        if slot == 0 and begin == 0:
            i = lax.broadcasted_iota(jnp.int32, chance.shape, 0)
            j = lax.broadcasted_iota(jnp.int32, chance.shape, 1)
            chance = chance - ((i == j) & (i < rows)).astype(jnp.float32)
        weights[here, begin * rows : end * rows] = (sharp * chance).astype(jnp.bfloat16)

    def image_grad(slot, count):
        here = pl.ds(slot * rows, count * rows)
        part_sum[here] = jnp.dot(weights[here], txt[...], preferred_element_type=jnp.float32)

    def text_grad(begin, end):
        tgrad[begin * rows : end * rows] = lax.dot_general(
            weights[:, begin * rows : end * rows], img[...], (((0,), (0,)), ((), ())),
            preferred_element_type=jnp.float32,
        )

    def take(slot, part):
        start, size = place(part)
        return part_rows(part_sum, slot, start, size)

    def part_rows(ref, slot, start, size):
        return ref[slot * rows + start : slot * rows + start + size]

    def put(slot, part, *extra):
        start, size = place(part)
        value = take(slot, part)
        for ref, ref_slot in extra:
            value = value + part_rows(ref, ref_slot, start, size).astype(jnp.float32)
        isend[slot * rows + start : slot * rows + start + size] = value.astype(jnp.bfloat16)

    @pl.when(low & (beyond > 0))
    def _():
        pl.semaphore_wait(barrier, beyond)

        @pl.when(across)
        def _():
            copies["tsecond"].start()

        @pl.when(far_across)
        def _():
            copies["tfar"].start()

    score(0, 4, 0, EARLY)

    arrived("partA+", "partA-")
    move("pfwdA+", "A0", img, 5, img, 7, up)
    move("pfwdA-", "A1", img, 4, img, 7, down)

    @pl.when(across & jnp.logical_not(low))
    def _():
        second_text()

    arrived("xB2", "xB3")
    score(4, 2, 0, EARLY)

    @pl.when(low & across)
    def _():
        second_text()

    arrived("tsib2")
    score(0, 4, EARLY, FAR)
    score(4, 2, EARLY, FAR)
    arrived("fwdA+", "fwdA-", "pfwdA+", "pfwdA-", "xB6")
    score(6, 2, 0, FAR)
    arrived("tfar")
    score(6, 2, FAR, TEXTS)
    image_grad(6, 2)
    put(7, "B")
    move("xsum7", "B", isend, 7, ixsum, 3, x_dev)
    put(7, "A")
    move("phalfA+", "A0", isend, 7, ihalf, 0, up)
    move("phalfA-", "A1", isend, 7, ihalf, 0, down)
    put(6, "A")
    move("halfA+", "A0", isend, 6, ihalf, 1, up)
    move("halfA-", "A1", isend, 6, ihalf, 1, down)

    def grad_rows(slot):
        return tgrad[slot * rows : (slot + 1) * rows]

    def put_text(n, value):
        tsend[n * rows : (n + 1) * rows] = value.astype(jnp.bfloat16)

    def got_text(n):
        return trecv[n * rows : (n + 1) * rows].astype(jnp.float32)

    score(0, 6, FAR, TEXTS)
    text_grad(FAR, TEXTS)
    put_text(6, grad_rows(6))
    send("gfar", block(tsend, 6), block(trecv, 5), far)
    text_grad(EARLY, FAR)
    put_text(5, grad_rows(5))
    send("gsib2", block(tsend, 5), block(trecv, 2), sibling)

    image_grad(4, 2)
    put(4, "B")
    move("xsum4", "B", isend, 4, ixsum, 1, x_dev)
    put(5, "B")
    move("xsum5", "B", isend, 5, ixsum, 2, x_dev)
    put(4, "A1")
    move("pfullA+1", "A1", isend, 4, ifull, 0, up)
    put(5, "A0")
    move("pfullA-0", "A0", isend, 5, ifull, 1, down)

    arrived("phalfA+", "phalfA-")
    put(4, "A0", (ihalf, 0))
    move("pfullA+0", "A0", isend, 4, ifull, 0, up)
    put(5, "A1", (ihalf, 0))
    move("pfullA-1", "A1", isend, 5, ifull, 1, down)

    image_grad(0, 4)
    put(1, "B")
    move("xsum1", "B", isend, 1, ixsum, 0, x_dev)
    put(2, "A1")
    move("fullA+1", "A1", isend, 2, ifull, 2, up)
    put(3, "A0")
    move("fullA-0", "A0", isend, 3, ifull, 3, down)
    arrived("halfA+", "halfA-")
    put(2, "A0", (ihalf, 1))
    move("fullA+0", "A0", isend, 2, ifull, 2, up)
    put(3, "A1", (ihalf, 1))
    move("fullA-1", "A1", isend, 3, ifull, 3, down)

    arrived("xsum7")
    put(6, "B", (ixsum, 3))
    move("halfB+", "B0", isend, 6, ihalf, 1, up)
    move("halfB-", "B1", isend, 6, ihalf, 1, down)

    def pass_back(name, slot, other, more):
        @pl.when(more)
        def _():
            arrived("gfar")
            put_text(slot, grad_rows(slot) + got_text(other) + got_text(5))

        @pl.when(jnp.logical_not(more))
        def _():
            put_text(slot, grad_rows(slot) + got_text(other))

        copies[name].start()

    make("gfirst", block(tsend, 2), block(trecv, 3 + at_first), first, at_first)
    make("gsecond", block(tsend, 4), block(trecv, 3 + at_second), second, at_second - 1)

    arrived("gsib2")
    pass_back("gsecond", 4, 2, jnp.logical_not(by_first))

    text_grad(0, EARLY)
    put_text(3, grad_rows(3))
    send("gsib1", block(tsend, 3), block(trecv, 1), sibling)
    put_text(1, grad_rows(1))
    send("gsib", block(tsend, 1), block(trecv, 0), sibling)

    arrived("pfullA+0", "pfullA+1", "pfullA-0", "pfullA-1")
    put(1, "A", (ifull, 0), (ifull, 1))
    move("xsumA", "A", isend, 1, ifull, 4, x_dev)

    arrived("gsib1")

    def pass_first():
        pass_back("gfirst", 2, 1, by_first)

    @pl.when(jnp.logical_not(low & far_across))
    def _():
        pass_first()

    arrived("xsum4", "xsum5", "halfB+", "halfB-")
    put(2, "B0", (ixsum, 1), (ihalf, 1))
    put(2, "B1", (ixsum, 1))
    move("fullB+", "B", isend, 2, ifull, 2, up)
    put(3, "B0", (ixsum, 2))
    put(3, "B1", (ixsum, 2), (ihalf, 1))
    move("fullB-", "B", isend, 3, ifull, 3, down)

    @pl.when(low & far_across)
    def _():
        pass_first()

    def got_full(n):
        return ifull[n * rows : (n + 1) * rows].astype(jnp.float32)

    arrived("gsib")
    def back(ref, grad):
        unit, inverse = unit_of(ref)
        return inverse * (grad - unit * jnp.sum(unit * grad, axis=-1, keepdims=True))

    arrived("fullA+0", "fullA+1", "fullA-0", "fullA-1", "xsumA", "xsum1", "fullB+", "fullB-")
    size = place("A")[1]
    crossed = (got_full(4)[:size], ixsum[size : 2 * size].astype(jnp.float32))
    pic_hat_grad = part_sum[0:rows] + got_full(2) + got_full(3) + jnp.concatenate(crossed, axis=0)
    pic_out[...] = back(pic, pic_hat_grad)

    came("gfirst", block(trecv, 3))
    tgrad[0:rows] = grad_rows(0) + got_text(0) + got_text(3)
    came("gsecond", block(trecv, 4))
    cap_out[...] = back(cap, grad_rows(0) + got_text(4))

    for name in COPIES:
        copies[name].wait_send()


def shards(picture_embedding_raw, caption_embedding_raw, score_sharpness, score_shift_term):
    rows, width = picture_embedding_raw.shape
    n_pool = lax.axis_size("pool")
    result = jax.ShapeDtypeStruct((rows, width), jnp.float32)

    def blocks(count, dtype=jnp.bfloat16):
        return pltpu.VMEM((count * rows, width), dtype)

    vmem = pl.BlockSpec(memory_space=pltpu.VMEM)
    smem = pl.BlockSpec(memory_space=pltpu.SMEM)
    return pl.pallas_call(
        kernel,
        out_shape=(result, result),
        in_specs=[smem, smem, vmem, vmem],
        out_specs=(vmem, vmem),
        scratch_shapes=[
            blocks(n_pool),
            blocks(TEXTS),
            pltpu.VMEM((n_pool * rows, TEXTS * rows), jnp.bfloat16),
            blocks(n_pool, jnp.float32),
            blocks(TEXTS, jnp.float32),
            blocks(n_pool),
            blocks(4),
            blocks(2),
            blocks(5),
            blocks(TEXTS),
            blocks(6),
            pltpu.SemaphoreType.DMA((len(COPIES),)),
            pltpu.SemaphoreType.DMA((len(COPIES),)),
        ],
        compiler_params=pltpu.CompilerParams(
            collective_id=0, has_side_effects=True, vmem_limit_bytes=40 * 2**20
        ),
    )(score_sharpness, score_shift_term, picture_embedding_raw, caption_embedding_raw)

def solution(mesh):
    return jax.shard_map(
        shards,
        mesh=mesh,
        in_specs=(P(("loop", "pool"), None), P(("loop", "pool"), None), P(), P()),
        out_specs=(P(("loop", "pool"), None), P(("loop", "pool"), None)),
        check_vma=False,
    )
```
